32 devices in a mesh: groups: 2 (over y), fsdp: 8 (over z, x), tp: 2 (over core).
Axes of the slice: x: 2, y: 2, z: 4, core: 2. Of those that a mesh axis runs over, the one named last changes fastest.
Arguments:
- tokens: bfloat16 [64, 8192], P(('groups', 'fsdp'), 'tp'), parts along dimension 0, may hold values from -6 to 6
- lengths: int32 [16], P(('groups', 'fsdp')), parts along dimension 0, may hold values from 1 to 4, as said below
- norm_gain: bfloat16 [8192], replicated, may hold values from 0.099609375 to 1.8984375
- gate_codes: bfloat16 [8192, 16384], P('fsdp', 'tp'), may hold values from -4 to 4
- gate_scales: bfloat16 [64, 128], P('fsdp', 'tp'), may hold values from 0.004486084 to 0.029907227
- up_codes: bfloat16 [8192, 16384], P('fsdp', 'tp'), may hold values from -4 to 4
- up_scales: bfloat16 [64, 128], P('fsdp', 'tp'), may hold values from 0.004486084 to 0.029907227
- down_codes: bfloat16 [8192, 16384], P('fsdp', 'tp'), may hold values from -4 to 4
- down_scales: bfloat16 [64, 128], P('fsdp', 'tp'), may hold values from 0.0029907227 to 0.021972656
- value_head: float32 [8192], P('tp'), may hold values from -0.0625 to 0.0625
Outputs:
- layer_out: bfloat16 [64, 8192], P(('groups', 'fsdp'), 'tp'), parts along dimension 0
- values: float32 [64], P(('groups', 'fsdp')), parts along dimension 0
The draws below stay inside these ranges and needn't reach their ends.
There are 2 independent parts, one for each index of `groups`. The reference program is written for one: setup_inputs(seed, part) draws one part's arguments, and reference() takes and returns one part's arrays. A program takes and returns all parts, laid end to end along the dimension named above; an argument that names none is the same for every part. Nothing has to cross between parts.
Inputs may be any that keep to these rules, and one draw needn't show every extreme that they name: `lengths`: some index of fsdp has all 4 rows live.
All inputs are finite; a program needn't handle non-finite values.
Results may differ from the reference program's by a relative error of at most 0.0094.
Values may be sent and summed in bfloat16 or wider, within the bound.
No kernel may reach another device: no remote copies, remote signals or barrier semaphores. Data moves between devices by JAX's collectives and lax.ppermute only.
A program may use at most 384 MiB of HBM per device.

```python
import math
import jax
import jax.numpy as jnp
from jax import lax

D = 8192
FF = 16384
TILE = 128
TOK_DEV = 4
TOKENS = 32
N_FSDP = 8


def draw_lengths(key, part):
    key = jax.random.fold_in(key, 11)
    first_key, second_key = jax.random.split(key)
    base = jax.random.randint(first_key, (N_FSDP,), 1, TOK_DEV + 1)
    chosen = jax.random.randint(second_key, (), 0, N_FSDP)
    return jnp.where(jnp.arange(N_FSDP) == chosen, TOK_DEV, base).astype(jnp.int32)


def level_of(key, shape, cuts, low, top_value):
    level, own = 1.0, jax.random.fold_in(key, 6)
    for axis_at, blocks in cuts:
        steps = jnp.exp(jax.random.uniform(jax.random.fold_in(own, axis_at), (blocks,), jnp.float32, low / len(cuts), top_value / len(cuts)))
        level = level * jnp.repeat(steps, shape[axis_at] // blocks).reshape([-1 if axis == axis_at else 1 for axis in range(len(shape))])
    return level


def gaussian(rng, shape, width, reach, cuts=(), held_as=jnp.bfloat16):
    loudness = level_of(rng, shape, cuts, -0.22, 0.18) if cuts else 1.0
    entries = jax.random.normal(rng, shape, jnp.float32) * width * loudness
    return jnp.minimum(jnp.maximum(entries, -reach), reach).astype(held_as)


def setup_inputs(seed: int = 0, part: int = 0) -> dict:
    keys = jax.random.split(jax.random.key(seed), 11)
    part_splits = jax.random.split(jax.random.fold_in(keys[10], part), 11)
    tokens = gaussian(part_splits[0], (TOKENS, D), 1.0, 6.0, ((0, 8), (1, 2)))
    lengths = draw_lengths(jax.random.fold_in(jax.random.fold_in(keys[10], part), 71), part)
    norm_gain = jnp.clip(1.0 + 0.18 * jax.random.normal(keys[2], (D,), jnp.float32), 0.099609375, 1.8984375).astype(jnp.bfloat16)
    gate_codes = gaussian(keys[3], (D, FF), 1.0, 4.0, ((0, 8), (1, 2)))
    gate_scales = jnp.clip(jnp.exp(math.log(0.029907227) - 1.89712 * jax.random.uniform(keys[4], (D // TILE, FF // TILE), jnp.float32) ** level_of(keys[4], (D // TILE, FF // TILE), ((0, 8), (1, 2)), -0.2, 0.2)), 0.004486084, 0.029907227).astype(jnp.bfloat16)
    up_codes = gaussian(keys[5], (D, FF), 1.0, 4.0, ((0, 8), (1, 2)))
    up_scales = jnp.clip(jnp.exp(math.log(0.029907227) - 1.89712 * jax.random.uniform(keys[6], (D // TILE, FF // TILE), jnp.float32) ** level_of(keys[6], (D // TILE, FF // TILE), ((0, 8), (1, 2)), -0.2, 0.2)), 0.004486084, 0.029907227).astype(jnp.bfloat16)
    down_codes = gaussian(keys[7], (D, FF), 1.0, 4.0, ((0, 8), (1, 2)))
    down_scales = jnp.clip(jnp.exp(math.log(0.021972656) - 1.9942837 * jax.random.uniform(keys[8], (D // TILE, FF // TILE), jnp.float32) ** level_of(keys[8], (D // TILE, FF // TILE), ((0, 8), (1, 2)), -0.2, 0.2)), 0.0029907227, 0.021972656).astype(jnp.bfloat16)
    value_head = gaussian(keys[9], (D,), D ** -0.5, 0.0625, ((0, 2),), jnp.float32)
    return dict(tokens=tokens, lengths=lengths, norm_gain=norm_gain, gate_codes=gate_codes, gate_scales=gate_scales, up_codes=up_codes, up_scales=up_scales, down_codes=down_codes, down_scales=down_scales, value_head=value_head)


def dequantize(codes, scales):
    blocks = codes.astype(jnp.float32).reshape(scales.shape[0], TILE, scales.shape[1], TILE)
    scaled = blocks * scales.astype(jnp.float32)[:, None, :, None]
    return scaled.reshape(codes.shape).astype(jnp.bfloat16)

def reference(tokens, lengths, norm_gain, gate_codes, gate_scales, up_codes, up_scales, down_codes, down_scales, value_head):
    resid = tokens.astype(jnp.float32)
    mean_sq = lax.optimization_barrier(jnp.mean(resid * resid, axis=-1, keepdims=True))
    normed = (resid * lax.rsqrt(mean_sq + 1e-05) * norm_gain.astype(jnp.float32)).astype(jnp.bfloat16)
    gate_act = jnp.dot(normed, dequantize(gate_codes, gate_scales), preferred_element_type=jnp.float32)
    up_act = jnp.dot(normed, dequantize(up_codes, up_scales), preferred_element_type=jnp.float32)
    hidden = (jax.nn.silu(gate_act) * up_act).astype(jnp.bfloat16)
    down_weight = dequantize(down_codes, down_scales)
    branch = lax.dot_general(hidden, down_weight, (((1,), (1,)), ((), ())), preferred_element_type=jnp.float32)
    layer_out = (resid + branch).astype(jnp.bfloat16)
    head = jnp.dot(layer_out.astype(jnp.float32), value_head, precision=lax.Precision.HIGHEST)
    position = jnp.arange(TOKENS) % TOK_DEV
    owner = jnp.arange(TOKENS) // TOK_DEV
    live = position < lengths[owner]
    values = jnp.where(live, head, jnp.float32(0.0))
    return (layer_out, values)
```

```python
import functools

import jax
import jax.numpy as jnp
from jax import lax
from jax.experimental import pallas as pl
from jax.experimental.pallas import tpu as pltpu
from jax.sharding import PartitionSpec as P

TILE = 128
BF16, F32 = jnp.bfloat16, jnp.float32
VMEM_SPEC = pl.BlockSpec(memory_space=pltpu.VMEM)
SMEM_SPEC = pl.BlockSpec(memory_space=pltpu.SMEM)


def params(mib):
    return pltpu.CompilerParams(vmem_limit_bytes=mib << 20)


def dequantize(codes, scales):
    tile_rows = codes.shape[0] // scales.shape[0]
    tile_cols = codes.shape[1] // scales.shape[1]
    blocks = codes.astype(F32).reshape(scales.shape[0], tile_rows, scales.shape[1], tile_cols)
    scaled = blocks * scales.astype(F32)[:, None, :, None]
    return scaled.reshape(codes.shape).astype(BF16)


def rms_normed(rows_in, norm_gain):
    resid = rows_in.astype(F32)
    mean_sq = jnp.mean(resid * resid, axis=-1, keepdims=True)
    return (resid * lax.rsqrt(mean_sq + 1e-05) * norm_gain.astype(F32)).astype(BF16)


def body_any(tokens, lengths, norm_gain, gate_codes, gate_scales, up_codes, up_scales, down_codes, down_scales, value_head):
    rows = tokens.shape[0]
    feature_rows = lax.all_gather(tokens, "tp", axis=1, tiled=True)
    normed = rms_normed(feature_rows, norm_gain)
    x = lax.all_to_all(normed, "fsdp", split_axis=1, concat_axis=0, tiled=True)
    gate = jnp.dot(x, dequantize(gate_codes, gate_scales), preferred_element_type=F32)
    up = jnp.dot(x, dequantize(up_codes, up_scales), preferred_element_type=F32)
    gate = lax.psum_scatter(gate, "fsdp", scatter_dimension=1, tiled=True)
    up = lax.psum_scatter(up, "fsdp", scatter_dimension=1, tiled=True)
    hidden = (jax.nn.silu(gate) * up).astype(BF16)
    hidden = lax.all_gather(hidden, "fsdp", axis=1, tiled=True)
    part = lax.dot_general(
        hidden, dequantize(down_codes, down_scales), (((1,), (1,)), ((), ())), preferred_element_type=F32
    )
    part = lax.all_to_all(part, "fsdp", split_axis=0, concat_axis=1, tiled=True)
    branch = lax.psum_scatter(part, "tp", scatter_dimension=1, tiled=True)
    layer_out = (tokens.astype(F32) + branch).astype(BF16)
    head = jnp.dot(layer_out.astype(F32), value_head, precision=lax.Precision.HIGHEST)
    head = lax.psum(head, "tp")
    live = jnp.arange(rows) < lengths[0]
    return layer_out, jnp.where(live, head, F32(0.0))


def norm_kernel(tok_ref, gain_ref, out_ref):
    n, _, width = out_ref.shape
    resid = tok_ref[...].astype(F32)
    mean_sq = jnp.mean(resid * resid, axis=-1, keepdims=True)
    inv = lax.rsqrt(mean_sq + 1e-05)
    gain = gain_ref[...].astype(F32)
    for c in range(n):
        cols = slice(c * width, (c + 1) * width)
        out_ref[c] = (resid[:, cols] * inv * gain[:, cols]).astype(BF16)


def gate_up_weights_kernel(g_ref, scl_ref, gate_ref, up_ref, out_ref):
    k, blocks, per = pl.program_id(0), out_ref.shape[0], out_ref.shape[2] // (2 * TILE)
    base = g_ref[0] * (blocks * per)
    rows = pl.ds(pl.multiple_of(k * TILE, TILE), TILE)
    for m, ref in enumerate((gate_ref, up_ref)):
        for b in range(blocks):
            for i in range(per):
                j = b * per + i
                scale = scl_ref[m, k, base + j]
                out_ref[b, rows, (m * per + i) * TILE : (m * per + i + 1) * TILE] = (
                    ref[:, j * TILE : (j + 1) * TILE].astype(F32) * scale
                ).astype(BF16)


def down_weights_kernel(g_ref, scl_ref, down_ref, out_ref):
    k, blocks, per = pl.program_id(0), out_ref.shape[0], out_ref.shape[2] // TILE
    base = g_ref[0] * (blocks * per)
    rows = pl.ds(pl.multiple_of(k * TILE, TILE), TILE)
    for b in range(blocks):
        for i in range(per):
            j = b * per + i
            scale = scl_ref[k, base + j]
            out_ref[b, rows, i * TILE : (i + 1) * TILE] = (
                down_ref[:, j * TILE : (j + 1) * TILE].astype(F32) * scale
            ).astype(BF16)


def gate_up_kernel(n, piece, me_ref, x_ref, w_ref, send_ref, keep_ref):
    me = me_ref[0]
    x = x_ref[...]
    for s in range(n // 2):
        for odd, ref in ((1, send_ref), (0, keep_ref)):
            block = piece * n + (me ^ (2 * s + odd))
            ref[s] = jnp.dot(x, w_ref[block], preferred_element_type=F32).astype(ref.dtype)


def pair_sum_kernel(keep_ref, got_ref, own_ref, *send_refs):
    own_ref[...] = keep_ref[0] + got_ref[0].astype(F32)
    for s, ref in enumerate(send_refs, 1):
        ref[...] = (keep_ref[s] + got_ref[s].astype(F32)).astype(BF16)


def hidden_kernel(own_ref, *refs):
    out_ref = refs[-1]
    total = own_ref[...]
    for ref in refs[:-1]:
        total = total + ref[...].astype(F32)
    half = out_ref.shape[-1]
    gate, up = total[:, :half], total[:, half:]
    out_ref[...] = (gate / (1.0 + jnp.exp(-gate)) * up).astype(BF16)


def down_kernel(n, piece, first, me_ref, *refs):
    near, far_ref = refs[: n // 2], refs[n // 2]
    w_ref, out_ref = refs[n // 2 + 1], refs[-1]
    me = me_ref[0]
    total = None if first else refs[n // 2 + 2][...]
    for s in range(n // 2):
        for odd in (0, 1):
            block = piece * n + (me ^ (2 * s + odd))
            h = far_ref[s] if odd else near[s][...]
            part = lax.dot_general(h, w_ref[block], (((1,), (1,)), ((), ())), preferred_element_type=F32)
            total = part if total is None else total + part
    out_ref[...] = total


def final_kernel(place_ref, tok_ref, branch_ref, head_ref, out_ref, values_ref):
    n, rows, width = branch_ref.shape
    half = out_ref.shape[1]
    total = jnp.zeros((rows, 1), F32)
    kept = []
    for c in range(n):
        cols = slice(c * width, (c + 1) * width)
        layer = (tok_ref[:, cols].astype(F32) + branch_ref[c].astype(F32)).astype(BF16)
        kept.append(layer)
        total = total + jnp.sum(layer.astype(F32) * head_ref[:, cols], axis=-1, keepdims=True)
    per = half // width
    for i in range(per):
        out_ref[:, i * width : (i + 1) * width] = jnp.where(place_ref[0] == 0, kept[i], kept[i + per])
    live = lax.broadcasted_iota(jnp.int32, (rows, 1), 0) < place_ref[1]
    values_ref[...] = jnp.broadcast_to(jnp.where(live, total, 0.0), values_ref.shape)


def body_split(pieces, n, tokens, lengths, norm_gain, gate_codes, gate_scales, up_codes, up_scales, down_codes, down_scales, value_head):
    rows, d_half = tokens.shape
    d, depth, ff_dev = 2 * d_half, gate_codes.shape[0], gate_codes.shape[1]
    group_cols = ff_dev // 2
    width = group_cols // (pieces * n)
    all_rows = 2 * n * rows
    half = n // 2
    me = lax.axis_index("fsdp").astype(jnp.int32).reshape(1)
    group = lax.axis_index("groups").astype(jnp.int32).reshape(1)
    core = lax.axis_index("tp").astype(jnp.int32)

    def swap(x, axis, bit):
        size = 2 if axis != "fsdp" else n
        return lax.ppermute(x, axis, [(i, i ^ bit) for i in range(size)])

    gu_scales = jnp.stack([gate_scales, up_scales]).astype(F32)
    w_gu = pl.pallas_call(
        gate_up_weights_kernel,
        grid_spec=pltpu.PrefetchScalarGridSpec(
            num_scalar_prefetch=1,
            grid=(depth // TILE,),
            in_specs=[
                SMEM_SPEC,
                pl.BlockSpec((TILE, group_cols), lambda k, g: (k, g[0])),
                pl.BlockSpec((TILE, group_cols), lambda k, g: (k, g[0])),
            ],
            out_specs=VMEM_SPEC,
        ),
        out_shape=pltpu.VMEM((pieces * n, depth, 2 * width), BF16),
        compiler_params=params(8),
        cost_estimate=pl.CostEstimate(flops=0, transcendentals=0, bytes_accessed=4 * depth * group_cols),
        name="gate_up_weights",
    )(group, gu_scales, gate_codes, up_codes)
    w_down = pl.pallas_call(
        down_weights_kernel,
        grid_spec=pltpu.PrefetchScalarGridSpec(
            num_scalar_prefetch=1,
            grid=(depth // TILE,),
            in_specs=[SMEM_SPEC, pl.BlockSpec((TILE, group_cols), lambda k, g: (k, g[0]))],
            out_specs=VMEM_SPEC,
        ),
        out_shape=pltpu.VMEM((pieces * n, depth, width), BF16),
        compiler_params=params(8),
        cost_estimate=pl.CostEstimate(flops=0, transcendentals=0, bytes_accessed=2 * depth * group_cols),
        name="down_weights",
    )(group, down_scales.astype(F32), down_codes)

    feature_rows = lax.all_gather(tokens, "tp", axis=1, tiled=True)
    head = lax.all_gather(value_head, "tp", axis=0, tiled=True)
    normed = pl.pallas_call(
        norm_kernel,
        out_shape=jax.ShapeDtypeStruct((n, rows, depth), BF16),
        name="norm",
    )(feature_rows, norm_gain.reshape(1, d))
    x_own = lax.all_to_all(normed, "fsdp", 0, 0, tiled=True).reshape(n * rows, depth)
    x = jnp.concatenate([x_own, swap(x_own, "groups", 1)], axis=0)

    branch = None
    for p in range(pieces):
        send, keep = pl.pallas_call(
            functools.partial(gate_up_kernel, n, p),
            in_specs=[SMEM_SPEC, VMEM_SPEC, VMEM_SPEC],
            out_specs=[VMEM_SPEC, VMEM_SPEC],
            out_shape=[
                jax.ShapeDtypeStruct((half, all_rows, 2 * width), BF16),
                jax.ShapeDtypeStruct((half, all_rows, 2 * width), F32),
            ],
            compiler_params=params(8),
            cost_estimate=pl.CostEstimate(
                flops=2 * all_rows * depth * 2 * width * n, transcendentals=0, bytes_accessed=4 * depth * width * n
            ),
            name=f"gate_up_{p}",
        )(me, x, pltpu.with_memory_space_constraint(w_gu, pltpu.VMEM))
        got = swap(send, "fsdp", 1)
        sums = pl.pallas_call(
            pair_sum_kernel,
            out_shape=[jax.ShapeDtypeStruct((all_rows, 2 * width), F32)]
            + [jax.ShapeDtypeStruct((all_rows, 2 * width), BF16)] * (half - 1),
            name=f"pair_sum_{p}",
        )(keep, got)
        got = [swap(sums[s], "fsdp", 2 * s) for s in range(1, half)]
        hidden = pl.pallas_call(
            hidden_kernel,
            out_shape=jax.ShapeDtypeStruct((all_rows, width), BF16),
            name=f"hidden_{p}",
        )(sums[0], *got)
        near = [hidden] + [swap(hidden, "fsdp", 2 * s) for s in range(1, half)]
        far = swap(jnp.stack(near), "fsdp", 1)
        before = [] if branch is None else [branch]
        branch = pl.pallas_call(
            functools.partial(down_kernel, n, p, branch is None),
            in_specs=[SMEM_SPEC] + [VMEM_SPEC] * (half + 2 + len(before)),
            out_specs=VMEM_SPEC,
            out_shape=jax.ShapeDtypeStruct((all_rows, depth), F32),
            compiler_params=params(8),
            cost_estimate=pl.CostEstimate(
                flops=2 * all_rows * depth * width * n, transcendentals=0, bytes_accessed=2 * depth * width * n
            ),
            name=f"down_{p}",
        )(me, *near, far, pltpu.with_memory_space_constraint(w_down, pltpu.VMEM), *before)

    branch = branch + swap(branch, "tp", 1)
    other = swap(branch[n * rows :].astype(BF16), "groups", 1)
    branch = (branch[: n * rows] + other.astype(F32)).astype(BF16)
    branch = lax.all_to_all(branch.reshape(n, rows, depth), "fsdp", 0, 0, tiled=True)
    place = jnp.stack([core, lengths[0]])
    layer_out, values = pl.pallas_call(
        final_kernel,
        in_specs=[SMEM_SPEC] + [VMEM_SPEC] * 3,
        out_specs=[VMEM_SPEC, VMEM_SPEC],
        out_shape=[jax.ShapeDtypeStruct((rows, d_half), BF16), jax.ShapeDtypeStruct((rows, TILE), F32)],
        name="final",
    )(place, feature_rows, branch, head.reshape(1, d))
    return layer_out, values[:, 0]


def solution(mesh):
    placed = (
        P(("groups", "fsdp"), "tp"),
        P(("groups", "fsdp")),
        P(),
        P("fsdp", "tp"),
        P("fsdp", "tp"),
        P("fsdp", "tp"),
        P("fsdp", "tp"),
        P("fsdp", "tp"),
        P("fsdp", "tp"),
        P("tp"),
    )
    n, pieces = mesh.shape["fsdp"], 2

    def body(*args):
        codes = args[3]
        fits = (
            n == 8
            and mesh.shape["groups"] == 2
            and mesh.shape["tp"] == 2
            and codes.shape[0] % TILE == 0
            and codes.shape[1] % (2 * pieces * n * TILE) == 0
        )
        if fits:
            return body_split(pieces, n, *args)
        return body_any(*args)

    return jax.shard_map(
        body,
        mesh=mesh,
        in_specs=placed,
        out_specs=(P(("groups", "fsdp"), "tp"), P(("groups", "fsdp"))),
        check_vma=False,
    )
```

```python
import functools

import jax
import jax.numpy as jnp
from jax import lax
from jax.experimental import pallas as pl
from jax.experimental.pallas import tpu as pltpu
from jax.sharding import PartitionSpec as P

TILE = 128
CODE_ROWS = 16
LOG2_E, LN_2 = 1.4426950408889634, 0.6931471805599453
BF16, F32 = jnp.bfloat16, jnp.float32
VMEM_SPEC = pl.BlockSpec(memory_space=pltpu.VMEM)
SMEM_SPEC = pl.BlockSpec(memory_space=pltpu.SMEM)


def params(mib):
    return pltpu.CompilerParams(vmem_limit_bytes=mib << 20)


def dequantize(codes, scales):
    tile_rows = codes.shape[0] // scales.shape[0]
    tile_cols = codes.shape[1] // scales.shape[1]
    blocks = codes.astype(F32).reshape(scales.shape[0], tile_rows, scales.shape[1], tile_cols)
    scaled = blocks * scales.astype(F32)[:, None, :, None]
    return scaled.reshape(codes.shape).astype(BF16)


def rms_normed(rows_in, norm_gain):
    resid = rows_in.astype(F32)
    mean_sq = jnp.mean(resid * resid, axis=-1, keepdims=True)
    return (resid * lax.rsqrt(mean_sq + 1e-05) * norm_gain.astype(F32)).astype(BF16)


def body_any(tokens, lengths, norm_gain, gate_codes, gate_scales, up_codes, up_scales, down_codes, down_scales, value_head):
    rows = tokens.shape[0]
    feature_rows = lax.all_gather(tokens, "tp", axis=1, tiled=True)
    normed = rms_normed(feature_rows, norm_gain)
    x = lax.all_to_all(normed, "fsdp", split_axis=1, concat_axis=0, tiled=True)
    gate = jnp.dot(x, dequantize(gate_codes, gate_scales), preferred_element_type=F32)
    up = jnp.dot(x, dequantize(up_codes, up_scales), preferred_element_type=F32)
    gate = lax.psum_scatter(gate, "fsdp", scatter_dimension=1, tiled=True)
    up = lax.psum_scatter(up, "fsdp", scatter_dimension=1, tiled=True)
    hidden = (jax.nn.silu(gate) * up).astype(BF16)
    hidden = lax.all_gather(hidden, "fsdp", axis=1, tiled=True)
    part = lax.dot_general(
        hidden, dequantize(down_codes, down_scales), (((1,), (1,)), ((), ())), preferred_element_type=F32
    )
    part = lax.all_to_all(part, "fsdp", split_axis=0, concat_axis=1, tiled=True)
    branch = lax.psum_scatter(part, "tp", scatter_dimension=1, tiled=True)
    layer_out = (tokens.astype(F32) + branch).astype(BF16)
    head = jnp.dot(layer_out.astype(F32), value_head, precision=lax.Precision.HIGHEST)
    head = lax.psum(head, "tp")
    live = jnp.arange(rows) < lengths[0]
    return layer_out, jnp.where(live, head, F32(0.0))


def norm_kernel(place_ref, mine_ref, core_mate_ref, group_mate_ref, far_mate_ref, gain_ref, *refs):
    out_ref, all_ref = refs[-2:]
    n, _, width = out_ref.shape
    rows, half = mine_ref.shape
    per = half // width
    core = place_ref[1]
    for at, halves in ((0, (mine_ref, core_mate_ref)), (rows, (group_mate_ref, far_mate_ref))):
        resid = [ref[...].astype(F32) for ref in halves]
        total = sum(jnp.sum(r * r, axis=-1, keepdims=True) for r in resid)
        inv = lax.rsqrt(total * (1.0 / (2 * half)) + 1e-05)
        for side, r in enumerate(resid):
            for i in range(per):
                c = (core ^ side) * per + i
                gain = gain_ref[:, pl.ds(pl.multiple_of(c * width, TILE), width)].astype(F32)
                all_ref[c, at : at + rows] = r[:, i * width : (i + 1) * width] * inv * gain
    out_ref[...] = all_ref[...].astype(BF16)


def encode(values, out_ref):
    count, rows = len(values), values[0].shape[0]
    top = functools.reduce(jnp.maximum, [jnp.max(jnp.abs(v), axis=0, keepdims=True) for v in values])
    power = jnp.clip(jnp.ceil(jnp.log(top) * LOG2_E), -100.0, 100.0)
    unit = jnp.exp((14.0 - power) * LN_2)
    for i, v in enumerate(values):
        out_ref[i * rows : (i + 1) * rows] = jnp.round(v * unit).astype(jnp.int32).astype(jnp.int16)
    tail = (out_ref.shape[0] - count * rows, out_ref.shape[1])
    out_ref[count * rows :] = jnp.broadcast_to(power.astype(jnp.int32), tail).astype(jnp.int16)


def decode(got_ref, rows, entries):
    count = (got_ref.shape[0] - CODE_ROWS) // rows
    power = got_ref[count * rows :].astype(jnp.int32).astype(F32)[:1]
    unit = jnp.exp((power - 14.0) * LN_2)
    return [got_ref[i * rows : (i + 1) * rows].astype(jnp.int32).astype(F32) * unit for i in entries]


def scaled(codes, scale_of, down, across):
    tiles = [
        [
            codes[r * TILE : (r + 1) * TILE, c * TILE : (c + 1) * TILE] * scale_of(r, c).astype(BF16)
            for c in range(across)
        ]
        for r in range(down)
    ]
    return jnp.concatenate([jnp.concatenate(row, axis=1) for row in tiles], axis=0)


def gate_up_kernel(piece, slots, first, place_ref, scl_ref, x_ref, gate_ref, up_ref, send_ref, keep_ref, sums_ref):
    me, group = place_ref[0], place_ref[3]
    x = x_ref[...].reshape(-1, x_ref.shape[-1])
    n, wide = 2 * len(slots), keep_ref.shape[-1] // 2
    units, step = wide // TILE, 2 * TILE
    for flip, out_ref in ((first, sums_ref), (0, keep_ref)):
        for i, slot in enumerate(slots):
            block = (group * 2 + piece) * n + (me ^ (slot ^ flip))
            cols = pl.ds(pl.multiple_of(block * wide, TILE), wide)
            for m, ref in enumerate((gate_ref, up_ref)):
                total = None
                for k in range(0, x.shape[1], step):
                    w = scaled(
                        ref[k : k + step, cols], lambda r, c: scl_ref[m, k // TILE + r, block * units + c], 2, units
                    )
                    part = jnp.dot(x[:, k : k + step], w, preferred_element_type=F32)
                    total = part if total is None else total + part
                out_ref[i, :, m * wide : (m + 1) * wide] = total
        if flip:
            encode([sums_ref[i] for i in range(len(slots))], send_ref)


def halve_kernel(keep_ref, got_ref, *refs):
    stay_ref, send_ref = refs[-2:]
    half, rows = stay_ref.shape[0], stay_ref.shape[1]
    got = decode(got_ref, rows, range(2 * half))
    for i in range(half):
        stay_ref[i] = keep_ref[i] + got[i]
    encode([keep_ref[half + i] + got[half + i] for i in range(half)], send_ref)


def hidden_kernel(keep_ref, got_ref, out_ref):
    total = keep_ref[0] + decode(got_ref, keep_ref.shape[1], (0,))[0]
    wide = out_ref.shape[-1]
    gate, up = total[:, :wide], total[:, wide:]
    out_ref[0] = (gate / (1.0 + jnp.exp(-gate)) * up).astype(BF16)


def join_kernel(mine_ref, got_ref, out_ref):
    count = mine_ref.shape[0]
    out_ref[:count] = mine_ref[...]
    out_ref[count:] = got_ref[...]


def down_kernel(piece, slots, begin, last, place_ref, scl_ref, hidden_ref, codes_ref, *refs):
    me, group = place_ref[0], place_ref[3]
    wide, depth, step = hidden_ref.shape[-1], codes_ref.shape[0], 2 * TILE
    units, n = wide // TILE, 2 * len(slots)
    for r in range(0, depth, step):
        total = None if begin else refs[0][:, r : r + step]
        for i, slot in enumerate(slots):
            block = (group * 2 + piece) * n + (me ^ slot)
            cols = pl.ds(pl.multiple_of(block * wide, TILE), wide)
            w = scaled(codes_ref[r : r + step, cols], lambda t, c: scl_ref[r // TILE + t, block * units + c], 2, units)
            part = lax.dot_general(hidden_ref[i], w, (((1,), (1,)), ((), ())), preferred_element_type=F32)
            total = part if total is None else total + part
        if not last:
            refs[-1][:, r : r + step] = total
            continue
        keep_ref, other_ref = refs[-2:]
        rows = keep_ref.shape[1]
        total = total.reshape(n, 2 * rows, step)
        keep_ref[:, :, r : r + step] = total[:, :rows]
        other_ref[:, :, r : r + step] = total[:, rows:].astype(BF16)


def branch_kernel(keep_ref, core_mate_ref, group_mate_ref, far_mate_ref, out_ref):
    near = keep_ref[...] + core_mate_ref[...]
    far = group_mate_ref[...].astype(F32) + far_mate_ref[...].astype(F32)
    out_ref[...] = (near + far).astype(BF16)


def final_kernel(place_ref, tok_ref, tok_mate_ref, branch_ref, head_ref, head_mate_ref, out_ref, values_ref):
    n, rows, width = branch_ref.shape
    per = out_ref.shape[1] // width
    core = place_ref[1]
    total = jnp.zeros((rows, 1), F32)
    for side, (tok, head) in enumerate(((tok_ref, head_ref), (tok_mate_ref, head_mate_ref))):
        for i in range(per):
            cols = slice(i * width, (i + 1) * width)
            branch = branch_ref[(core ^ side) * per + i].astype(F32)
            layer = (tok[:, cols].astype(F32) + branch).astype(BF16)
            if side == 0:
                out_ref[:, cols] = layer
            total = total + jnp.sum(layer.astype(F32) * head[:, cols], axis=-1, keepdims=True)
    row, at = (lax.broadcasted_iota(jnp.int32, (rows, rows), axis) for axis in (0, 1))
    taken = (row == at) & (row < place_ref[2])
    values_ref[...] = jnp.sum(jnp.where(taken, total, 0.0), axis=0, keepdims=True)


def call(kernel, name, ins, outs, limit=8, cost=None, scratch=()):
    specs = [x[1] if isinstance(x, tuple) else VMEM_SPEC for x in ins]
    return pl.pallas_call(
        kernel,
        in_specs=specs,
        out_specs=jax.tree.map(lambda _: VMEM_SPEC, outs),
        out_shape=outs,
        scratch_shapes=scratch,
        compiler_params=params(limit),
        cost_estimate=cost,
        name=name,
    )(*[x[0] if isinstance(x, tuple) else x for x in ins])


def body_split(n, tokens, lengths, norm_gain, gate_codes, gate_scales, up_codes, up_scales, down_codes, down_scales, value_head):
    rows, d_half = tokens.shape
    d, depth = 2 * d_half, gate_codes.shape[0]
    group_cols = gate_codes.shape[1] // 2
    units = group_cols // (2 * n * TILE)
    all_rows, half = 2 * n * rows, n // 2
    me, group, core = (lax.axis_index(a).astype(jnp.int32) for a in ("fsdp", "groups", "tp"))
    place = jnp.stack([me, core, lengths[0], group])
    spot = (place, SMEM_SPEC)
    shape = jax.ShapeDtypeStruct

    def swap(x, axis, bit):
        size = n if axis == "fsdp" else 2 if isinstance(axis, str) else 4
        return lax.ppermute(x, axis, [(i, i ^ bit) for i in range(size)])

    def three(to_core, to_group, to_far):
        return swap(to_core, "tp", 1), swap(to_group, "groups", 1), swap(to_far, ("groups", "tp"), 3)

    hbm = lambda x: pltpu.with_memory_space_constraint(x, pltpu.HBM)
    vmem = lambda x: pltpu.with_memory_space_constraint(x, pltpu.VMEM)
    unread = lambda x: (x, pl.BlockSpec(memory_space=pl.ANY))

    gu_scales = jnp.stack([gate_scales, up_scales]).astype(F32)
    down_scales = down_scales.astype(F32)

    mates = three(tokens, tokens, tokens)
    head = value_head.reshape(1, d_half)
    head_mate = swap(head, "tp", 1)
    normed = call(
        norm_kernel,
        "norm",
        [spot, tokens, *mates, norm_gain.reshape(1, d)]
        + [unread(a) for a in (head_mate, gu_scales, down_scales)]
        + [unread(hbm(a)) for a in (gate_codes, up_codes, down_codes)],
        shape((n, 2 * rows, depth), BF16),
        scratch=[pltpu.VMEM((n, 2 * rows, depth), F32)],
    )
    x = lax.all_to_all(normed, "fsdp", 0, 0, tiled=True)

    wide = units * TILE
    codes = [vmem(c) for c in (gate_codes, up_codes)]
    cost = lambda share, width: pl.CostEstimate(
        flops=2 * all_rows * depth * width * n // share, transcendentals=0, bytes_accessed=2 * depth * width * n // share
    )

    coded = lambda count: shape((count * all_rows + CODE_ROWS, 2 * wide), jnp.int16)

    plans = ((1, 2, 4), (2, 1, 4))
    sent = []
    for p, (b1, b2, b3) in enumerate(plans):
        slots = (0, b3, b2, b2 ^ b3)
        send, keep = call(
            functools.partial(gate_up_kernel, p, slots, b1),
            f"gate_up_{p}",
            [spot, (gu_scales, SMEM_SPEC), x, *codes],
            [coded(half), shape((half, all_rows, 2 * wide), F32)],
            cost=cost(1, 2 * wide),
            scratch=[pltpu.VMEM((half, all_rows, 2 * wide), F32)],
        )
        sent.append((keep, swap(send, "fsdp", b1)))
    branch = None
    for p, (b1, b2, b3) in enumerate(plans):
        keep, got = sent[p]
        for count, bit in ((half // 2, b2), (half // 4, b3)):
            keep, send = call(
                halve_kernel,
                f"halve_{count}_{p}",
                [keep, got, unread(hbm(down_codes))],
                [shape((count, all_rows, 2 * wide), F32), coded(count)],
            )
            got = swap(send, "fsdp", bit)
        hidden = call(hidden_kernel, f"hidden_{p}", [keep, got], shape((1, all_rows, wide), BF16))
        for count, bit in ((2, b3), (4, b2)):
            got = swap(hidden, "fsdp", bit)
            hidden = call(join_kernel, f"join_{count}_{p}", [hidden, got], shape((count, all_rows, wide), BF16))
        slots = (0, b3, b2, b2 ^ b3)
        for part, flip in ((hidden, 0), (swap(hidden, "fsdp", b1), b1)):
            last = p == len(plans) - 1 and flip
            branch = call(
                functools.partial(down_kernel, p, tuple(s ^ flip for s in slots), branch is None, last),
                f"down_{p}_{min(flip, 1)}",
                [spot, (down_scales, SMEM_SPEC), part, vmem(down_codes)] + ([] if branch is None else [branch]),
                [shape((n, rows, depth), t) for t in (F32, BF16)] if last else shape((all_rows, depth), F32),
                cost=cost(2, wide),
            )

    keep, other = branch
    branch = call(branch_kernel, "branch", [keep, *three(keep, other, other)], shape((n, rows, depth), BF16))
    branch = lax.all_to_all(branch, "fsdp", 0, 0, tiled=True)
    layer_out, values = call(
        final_kernel,
        "final",
        [spot, tokens, mates[0], branch, head, head_mate],
        [shape((rows, d_half), BF16), shape((1, rows), F32)],
    )
    return layer_out, values.reshape(rows)


def solution(mesh):
    placed = (
        P(("groups", "fsdp"), "tp"),
        P(("groups", "fsdp")),
        P(),
        P("fsdp", "tp"),
        P("fsdp", "tp"),
        P("fsdp", "tp"),
        P("fsdp", "tp"),
        P("fsdp", "tp"),
        P("fsdp", "tp"),
        P("tp"),
    )
    n = mesh.shape["fsdp"]

    def body(*args):
        codes = args[3]
        fits = (
            n == 8
            and mesh.shape["groups"] == 2
            and mesh.shape["tp"] == 2
            and codes.shape[0] % TILE == 0
            and codes.shape[1] == 8 * n * TILE
        )
        if fits:
            return body_split(n, *args)
        return body_any(*args)

    return jax.shard_map(
        body,
        mesh=mesh,
        in_specs=placed,
        out_specs=(P(("groups", "fsdp"), "tp"), P(("groups", "fsdp"))),
        check_vma=False,
    )
```

```python
import functools

import jax
import jax.numpy as jnp
from jax import lax
from jax.experimental import pallas as pl
from jax.experimental.pallas import tpu as pltpu
from jax.sharding import PartitionSpec as P

TILE = 128
CODE_ROWS = 16
LOG2_E, LN_2 = 1.4426950408889634, 0.6931471805599453
BF16, F32 = jnp.bfloat16, jnp.float32
VMEM_SPEC = pl.BlockSpec(memory_space=pltpu.VMEM)
SMEM_SPEC = pl.BlockSpec(memory_space=pltpu.SMEM)


def params(mib):
    return pltpu.CompilerParams(vmem_limit_bytes=mib << 20)


def dequantize(codes, scales):
    tile_rows = codes.shape[0] // scales.shape[0]
    tile_cols = codes.shape[1] // scales.shape[1]
    blocks = codes.astype(F32).reshape(scales.shape[0], tile_rows, scales.shape[1], tile_cols)
    scaled = blocks * scales.astype(F32)[:, None, :, None]
    return scaled.reshape(codes.shape).astype(BF16)


def rms_normed(rows_in, norm_gain):
    resid = rows_in.astype(F32)
    mean_sq = jnp.mean(resid * resid, axis=-1, keepdims=True)
    return (resid * lax.rsqrt(mean_sq + 1e-05) * norm_gain.astype(F32)).astype(BF16)


def body_any(tokens, lengths, norm_gain, gate_codes, gate_scales, up_codes, up_scales, down_codes, down_scales, value_head):
    rows = tokens.shape[0]
    feature_rows = lax.all_gather(tokens, "tp", axis=1, tiled=True)
    normed = rms_normed(feature_rows, norm_gain)
    x = lax.all_to_all(normed, "fsdp", split_axis=1, concat_axis=0, tiled=True)
    gate = jnp.dot(x, dequantize(gate_codes, gate_scales), preferred_element_type=F32)
    up = jnp.dot(x, dequantize(up_codes, up_scales), preferred_element_type=F32)
    gate = lax.psum_scatter(gate, "fsdp", scatter_dimension=1, tiled=True)
    up = lax.psum_scatter(up, "fsdp", scatter_dimension=1, tiled=True)
    hidden = (jax.nn.silu(gate) * up).astype(BF16)
    hidden = lax.all_gather(hidden, "fsdp", axis=1, tiled=True)
    part = lax.dot_general(
        hidden, dequantize(down_codes, down_scales), (((1,), (1,)), ((), ())), preferred_element_type=F32
    )
    part = lax.all_to_all(part, "fsdp", split_axis=0, concat_axis=1, tiled=True)
    branch = lax.psum_scatter(part, "tp", scatter_dimension=1, tiled=True)
    layer_out = (tokens.astype(F32) + branch).astype(BF16)
    head = jnp.dot(layer_out.astype(F32), value_head, precision=lax.Precision.HIGHEST)
    head = lax.psum(head, "tp")
    live = jnp.arange(rows) < lengths[0]
    return layer_out, jnp.where(live, head, F32(0.0))


def norm_kernel(place_ref, mine_ref, core_mate_ref, gain_ref, gate_scl_ref, up_scl_ref, down_scl_ref, *refs):
    out_ref, gu_out_ref, down_out_ref = refs[-3:]
    gu_out_ref[0] = gate_scl_ref[...].astype(F32)
    gu_out_ref[1] = up_scl_ref[...].astype(F32)
    down_out_ref[...] = down_scl_ref[...].astype(F32)
    _, rows, width = out_ref.shape
    n = gain_ref.shape[0] // width
    per = mine_ref.shape[1] // width
    resid = [ref[...].astype(F32) for ref in (mine_ref, core_mate_ref)]
    total = sum(jnp.sum(r * r, axis=-1, keepdims=True) for r in resid)
    inv = lax.rsqrt(total * (1.0 / (n * width)) + 1e-05)
    for side, r in enumerate(resid):
        for i in range(per):
            c = (place_ref[1] ^ side) * per + i
            gain = gain_ref[pl.ds(pl.multiple_of(c * width, TILE), width)].astype(F32).reshape(1, width)
            chunk = (r[:, i * width : (i + 1) * width] * inv * gain).astype(BF16)
            for g in range(2):
                out_ref[g * n + c] = chunk


def hold_kernel(ref, *refs):
    refs[-1][...] = ref[...]


def rows_kernel(got_ref, out_ref, rows_ref):
    count, rows, _ = got_ref.shape
    for j in range(count):
        rows_ref[j * rows : (j + 1) * rows] = got_ref[j].astype(F32)
    out_ref[...] = rows_ref[...].astype(BF16)


def encode(values, out_ref):
    count, rows = len(values), values[0].shape[0]
    top = functools.reduce(jnp.maximum, [jnp.max(jnp.abs(v), axis=0, keepdims=True) for v in values])
    power = jnp.clip(jnp.ceil(jnp.log(top) * LOG2_E), -100.0, 100.0)
    unit = jnp.exp((14.0 - power) * LN_2)
    for i, v in enumerate(values):
        out_ref[i * rows : (i + 1) * rows] = jnp.round(v * unit).astype(jnp.int32).astype(jnp.int16)
    tail = (out_ref.shape[0] - count * rows, out_ref.shape[1])
    out_ref[count * rows :] = jnp.broadcast_to(power.astype(jnp.int32), tail).astype(jnp.int16)


def decode(got_ref, rows, entries):
    count = (got_ref.shape[0] - CODE_ROWS) // rows
    power = got_ref[count * rows :].astype(jnp.int32).astype(F32)[:1]
    unit = jnp.exp((power - 14.0) * LN_2)
    return [got_ref[i * rows : (i + 1) * rows].astype(jnp.int32).astype(F32) * unit for i in entries]


def scaled(codes, scale_of, down, across):
    tiles = [
        [
            codes[r * TILE : (r + 1) * TILE, c * TILE : (c + 1) * TILE] * scale_of(r, c).astype(BF16)
            for c in range(across)
        ]
        for r in range(down)
    ]
    return jnp.concatenate([jnp.concatenate(row, axis=1) for row in tiles], axis=0)


def gate_up_kernel(blocks, n, place_ref, scl_ref, x_ref, gate_ref, up_ref, _, *refs):
    me, group = place_ref[0], place_ref[3]
    x = x_ref[...]
    sums_ref = refs[-1]
    wide = sums_ref.shape[-1] // 2
    units, step = wide // TILE, 2 * TILE
    for (piece, q), out_ref in zip(blocks, refs):
        total_ref = sums_ref if q else out_ref
        for i in range(2):
            block = (group * 2 + piece) * n + (me ^ (q + i * (n // 2)))
            cols = pl.ds(pl.multiple_of(block * wide, TILE), wide)
            for m, ref in enumerate((gate_ref, up_ref)):
                total = None
                for k in range(0, x.shape[1], step):
                    w = scaled(
                        ref[k : k + step, cols], lambda r, c: scl_ref[m, k // TILE + r, block * units + c], 2, units
                    )
                    part = jnp.dot(x[:, k : k + step], w, preferred_element_type=F32)
                    total = part if total is None else total + part
                total_ref[i, :, m * wide : (m + 1) * wide] = total
        if q:
            encode([total_ref[i] for i in range(2)], out_ref)


def both_kernel(keep_ref, *refs):
    got_refs, (stay_ref, send_ref) = refs[:3], refs[-2:]
    count, rows = stay_ref.shape[0], stay_ref.shape[1]
    total = [keep_ref[i] for i in range(count)]
    for ref in got_refs:
        total = [t + v for t, v in zip(total, decode(ref, rows, range(count)))]
    for i in range(count):
        stay_ref[i] = total[i]
    encode(total, send_ref)


def hidden_kernel(keep_ref, got_ref, out_ref):
    count, wide = out_ref.shape[0], out_ref.shape[-1]
    got = decode(got_ref, keep_ref.shape[1], range(count))
    for i in range(count):
        total = keep_ref[i] + got[count - 1 - i]
        gate, up = total[:, :wide], total[:, wide:]
        out_ref[i] = (gate / (1.0 + jnp.exp(-gate)) * up).astype(BF16)


def down_kernel(piece, blocks, n, begin, last, place_ref, scl_ref, codes_ref, *refs):
    me, group = place_ref[0], place_ref[3]
    hidden_refs, out_ref = refs[: len(blocks)], refs[-1]
    wide, depth, step = hidden_refs[0].shape[-1], codes_ref.shape[0], 2 * TILE
    units = wide // TILE
    for r in range(0, depth, step):
        total = None if begin else refs[len(blocks)][:, r : r + step]
        for q, hidden_ref in zip(blocks, hidden_refs):
            for i in range(2):
                block = (group * 2 + piece) * n + (me ^ (q + i * (n // 2)))
                cols = pl.ds(pl.multiple_of(block * wide, TILE), wide)
                w = scaled(codes_ref[r : r + step, cols], lambda t, c: scl_ref[r // TILE + t, block * units + c], 2, units)
                part = lax.dot_general(hidden_ref[i], w, (((1,), (1,)), ((), ())), preferred_element_type=F32)
                total = part if total is None else total + part
        if not last:
            out_ref[:, r : r + step] = total
            continue
        count, rows, _ = out_ref.shape
        for j in range(count):
            out_ref[j, :, r : r + step] = total[j * rows : (j + 1) * rows].astype(BF16)


def group_sum_kernel(got_ref, out_ref):
    n = out_ref.shape[0]
    for c in range(n):
        out_ref[c] = got_ref[c].astype(F32) + got_ref[n + c].astype(F32)


def final_kernel(place_ref, tok_ref, tok_mate_ref, branch_ref, branch_mate_ref, head_ref, head_mate_ref, out_ref, values_ref):
    n, rows, width = branch_ref.shape
    per = out_ref.shape[1] // width
    core = place_ref[1]
    total = jnp.zeros((rows, 1), F32)
    for side, (tok, head) in enumerate(((tok_ref, head_ref), (tok_mate_ref, head_mate_ref))):
        for i in range(per):
            cols = slice(i * width, (i + 1) * width)
            c = (core ^ side) * per + i
            branch = branch_ref[c] + branch_mate_ref[c]
            layer = (tok[:, cols].astype(F32) + branch).astype(BF16)
            if side == 0:
                out_ref[:, cols] = layer
            total = total + jnp.sum(layer.astype(F32) * head[:, cols], axis=-1, keepdims=True)
    row, at = (lax.broadcasted_iota(jnp.int32, (rows, rows), axis) for axis in (0, 1))
    taken = (row == at) & (row < place_ref[2])
    values_ref[...] = jnp.sum(jnp.where(taken, total, 0.0), axis=0, keepdims=True)


def call(kernel, name, ins, outs, limit=8, cost=None, scratch=()):
    specs = [x[1] if isinstance(x, tuple) else VMEM_SPEC for x in ins]
    return pl.pallas_call(
        kernel,
        in_specs=specs,
        out_specs=jax.tree.map(lambda _: VMEM_SPEC, outs),
        out_shape=outs,
        scratch_shapes=scratch,
        compiler_params=params(limit),
        cost_estimate=cost,
        name=name,
    )(*[x[0] if isinstance(x, tuple) else x for x in ins])


def body_split(n, tokens, lengths, norm_gain, gate_codes, gate_scales, up_codes, up_scales, down_codes, down_scales, value_head):
    rows, d_half = tokens.shape
    d, depth = 2 * d_half, gate_codes.shape[0]
    group_cols = gate_codes.shape[1] // 2
    units = group_cols // (2 * n * TILE)
    all_rows, half = 2 * n * rows, n // 2
    me, group, core = (lax.axis_index(a).astype(jnp.int32) for a in ("fsdp", "groups", "tp"))
    place = jnp.stack([me, core, lengths[0], group])
    spot = (place, SMEM_SPEC)
    shape = jax.ShapeDtypeStruct

    def swap(x, axis, bit):
        return lax.ppermute(x, axis, [(i, i ^ bit) for i in range(n if axis == "fsdp" else 2)])

    hbm = lambda x: pltpu.with_memory_space_constraint(x, pltpu.HBM)
    vmem = lambda x: pltpu.with_memory_space_constraint(x, pltpu.VMEM)
    unread = lambda x: (x, pl.BlockSpec(memory_space=pl.ANY))

    tok_mate = swap(tokens, "tp", 1)
    head = value_head.reshape(1, d_half)
    head_mate = swap(head, "tp", 1)
    whole = lambda x: (hbm(x), pl.BlockSpec())
    normed, gu_scales, down_scales = call(
        norm_kernel,
        "norm",
        [spot, whole(tokens), tok_mate]
        + [whole(a) for a in (norm_gain, gate_scales, up_scales, down_scales)]
        + [unread(head_mate)],
        [
            shape((2 * n, rows, depth), BF16),
            shape((2, *gate_scales.shape), F32),
            shape(down_scales.shape, F32),
        ],
    )
    normed = call(
        hold_kernel,
        "hold",
        [normed] + [unread(hbm(a)) for a in (gate_codes, up_codes, down_codes)],
        shape(normed.shape, BF16),
    )
    both = ("groups", "fsdp")
    x = call(
        rows_kernel,
        "rows",
        [lax.all_to_all(normed, both, 0, 0, tiled=True)],
        shape((all_rows, depth), BF16),
        scratch=[pltpu.VMEM((all_rows, depth), F32)],
    )

    wide = units * TILE
    codes = [vmem(c) for c in (gate_codes, up_codes)]
    cost = lambda share, width: pl.CostEstimate(
        flops=2 * all_rows * depth * width * n // share, transcendentals=0, bytes_accessed=2 * depth * width * n // share
    )

    coded = lambda count: shape((count * all_rows + CODE_ROWS, 2 * wide), jnp.int16)

    far = n // 2
    sums = shape((2, all_rows, 2 * wide), F32)

    def gate_up(name, after, *blocks):
        return call(
            functools.partial(gate_up_kernel, blocks, n),
            f"gate_up_{name}",
            [spot, (gu_scales, SMEM_SPEC), x, *codes, unread(after)],
            [coded(2) if q else sums for _, q in blocks],
            cost=cost(2, 2 * wide),
            scratch=[pltpu.VMEM(sums.shape, F32)],
        )

    orders = ((1, 3, 2), (2, 3, 1))
    kept, got, after = [], [], x
    for p, (q1, q2, q3) in enumerate(orders):
        send_1, send_2 = gate_up(f"{p}_first", after, (p, q1), (p, q2))
        send_3, keep = gate_up(f"{p}_second", send_1, (p, q3), (p, 0))
        got.append([swap(send, "fsdp", q) for send, q in ((send_1, q1), (send_2, q2), (send_3, q3))])
        kept.append(keep)
        after = send_3
    branch = None
    for p, order in enumerate(orders):
        late = [unread(hbm(down_codes))] if p else []
        keep, send = call(both_kernel, f"both_{p}", [kept[p], *got[p], *late], [sums, coded(2)])
        hidden = call(hidden_kernel, f"hidden_{p}", [keep, swap(send, "fsdp", far)], shape((2, all_rows, wide), BF16))
        parts = [hidden] + [swap(hidden, "fsdp", q) for q in order]
        for at in ((0, 1), (1, 4)) if p else ((0, 4),):
            last = p == 1 and at[1] == 4
            branch = call(
                functools.partial(down_kernel, p, (0, *order)[slice(*at)], n, branch is None, last),
                f"down_{p}_{at[0]}",
                [spot, (down_scales, SMEM_SPEC), vmem(down_codes), *parts[slice(*at)]]
                + ([] if branch is None else [branch]),
                shape((2 * n, rows, depth), BF16) if last else shape((all_rows, depth), F32),
                cost=cost(2, wide),
            )

    got = lax.all_to_all(branch, both, 0, 0, tiled=True)
    branch = call(group_sum_kernel, "group_sum", [got], shape((n, rows, depth), F32))
    layer_out, values = call(
        final_kernel,
        "final",
        [spot, tokens, tok_mate, branch, swap(branch, "tp", 1), head, head_mate],
        [shape((rows, d_half), BF16), shape((1, rows), F32)],
    )
    return layer_out, values.reshape(rows)


def solution(mesh):
    placed = (
        P(("groups", "fsdp"), "tp"),
        P(("groups", "fsdp")),
        P(),
        P("fsdp", "tp"),
        P("fsdp", "tp"),
        P("fsdp", "tp"),
        P("fsdp", "tp"),
        P("fsdp", "tp"),
        P("fsdp", "tp"),
        P("tp"),
    )
    n = mesh.shape["fsdp"]

    def body(*args):
        codes = args[3]
        fits = (
            n == 8
            and mesh.shape["groups"] == 2
            and mesh.shape["tp"] == 2
            and codes.shape[0] % TILE == 0
            and codes.shape[1] == 8 * n * TILE
        )
        if fits:
            return body_split(n, *args)
        return body_any(*args)

    return jax.shard_map(
        body,
        mesh=mesh,
        in_specs=placed,
        out_specs=(P(("groups", "fsdp"), "tp"), P(("groups", "fsdp"))),
        check_vma=False,
    )
```

```python
import functools

import jax
import jax.numpy as jnp
from jax import lax
from jax.experimental import pallas as pl
from jax.experimental.pallas import tpu as pltpu
from jax.sharding import PartitionSpec as P

TILE = 128
CODE_ROWS = 16
LOG2_E, LN_2 = 1.4426950408889634, 0.6931471805599453
BF16, F32 = jnp.bfloat16, jnp.float32
VMEM_SPEC = pl.BlockSpec(memory_space=pltpu.VMEM)
SMEM_SPEC = pl.BlockSpec(memory_space=pltpu.SMEM)


def params(mib):
    return pltpu.CompilerParams(vmem_limit_bytes=mib << 20)


def dequantize(codes, scales):
    tile_rows = codes.shape[0] // scales.shape[0]
    tile_cols = codes.shape[1] // scales.shape[1]
    blocks = codes.astype(F32).reshape(scales.shape[0], tile_rows, scales.shape[1], tile_cols)
    scaled = blocks * scales.astype(F32)[:, None, :, None]
    return scaled.reshape(codes.shape).astype(BF16)


def rms_normed(rows_in, norm_gain):
    resid = rows_in.astype(F32)
    mean_sq = jnp.mean(resid * resid, axis=-1, keepdims=True)
    return (resid * lax.rsqrt(mean_sq + 1e-05) * norm_gain.astype(F32)).astype(BF16)


def body_any(tokens, lengths, norm_gain, gate_codes, gate_scales, up_codes, up_scales, down_codes, down_scales, value_head):
    rows = tokens.shape[0]
    feature_rows = lax.all_gather(tokens, "tp", axis=1, tiled=True)
    normed = rms_normed(feature_rows, norm_gain)
    x = lax.all_to_all(normed, "fsdp", split_axis=1, concat_axis=0, tiled=True)
    gate = jnp.dot(x, dequantize(gate_codes, gate_scales), preferred_element_type=F32)
    up = jnp.dot(x, dequantize(up_codes, up_scales), preferred_element_type=F32)
    gate = lax.psum_scatter(gate, "fsdp", scatter_dimension=1, tiled=True)
    up = lax.psum_scatter(up, "fsdp", scatter_dimension=1, tiled=True)
    hidden = (jax.nn.silu(gate) * up).astype(BF16)
    hidden = lax.all_gather(hidden, "fsdp", axis=1, tiled=True)
    part = lax.dot_general(
        hidden, dequantize(down_codes, down_scales), (((1,), (1,)), ((), ())), preferred_element_type=F32
    )
    part = lax.all_to_all(part, "fsdp", split_axis=0, concat_axis=1, tiled=True)
    branch = lax.psum_scatter(part, "tp", scatter_dimension=1, tiled=True)
    layer_out = (tokens.astype(F32) + branch).astype(BF16)
    head = jnp.dot(layer_out.astype(F32), value_head, precision=lax.Precision.HIGHEST)
    head = lax.psum(head, "tp")
    live = jnp.arange(rows) < lengths[0]
    return layer_out, jnp.where(live, head, F32(0.0))


def norm_kernel(place_ref, mine_ref, core_mate_ref, gain_ref, gate_scl_ref, up_scl_ref, down_scl_ref, *refs):
    out_ref, gu_out_ref, down_out_ref = refs[-3:]
    gu_out_ref[0] = gate_scl_ref[...].astype(F32)
    gu_out_ref[1] = up_scl_ref[...].astype(F32)
    down_out_ref[...] = down_scl_ref[...].astype(F32)
    _, rows, width = out_ref.shape
    n = gain_ref.shape[0] // width
    per = mine_ref.shape[1] // width
    resid = [ref[...].astype(F32) for ref in (mine_ref, core_mate_ref)]
    total = sum(jnp.sum(r * r, axis=-1, keepdims=True) for r in resid)
    inv = lax.rsqrt(total * (1.0 / (n * width)) + 1e-05)
    for side, r in enumerate(resid):
        for i in range(per):
            c = (place_ref[1] ^ side) * per + i
            gain = gain_ref[pl.ds(pl.multiple_of(c * width, TILE), width)].astype(F32).reshape(1, width)
            chunk = (r[:, i * width : (i + 1) * width] * inv * gain).astype(BF16)
            for g in range(2):
                out_ref[g * n + c] = chunk


def hold_kernel(ref, *refs):
    refs[-1][...] = ref[...]


def rows_kernel(got_ref, out_ref, rows_ref):
    count, rows, _ = got_ref.shape
    for j in range(count):
        rows_ref[j * rows : (j + 1) * rows] = got_ref[j].astype(F32)
    out_ref[...] = rows_ref[...].astype(BF16)


def encode(values, out_ref):
    count, rows = len(values), values[0].shape[0]
    top = functools.reduce(jnp.maximum, [jnp.max(jnp.abs(v), axis=0, keepdims=True) for v in values])
    power = jnp.clip(jnp.ceil(jnp.log(top) * LOG2_E), -100.0, 100.0)
    unit = jnp.exp((14.0 - power) * LN_2)
    for i, v in enumerate(values):
        out_ref[i * rows : (i + 1) * rows] = jnp.round(v * unit).astype(jnp.int32).astype(jnp.int16)
    tail = (out_ref.shape[0] - count * rows, out_ref.shape[1])
    out_ref[count * rows :] = jnp.broadcast_to(power.astype(jnp.int32), tail).astype(jnp.int16)


def decode(got_ref, rows, entries):
    count = (got_ref.shape[0] - CODE_ROWS) // rows
    power = got_ref[count * rows :].astype(jnp.int32).astype(F32)[:1]
    unit = jnp.exp((power - 14.0) * LN_2)
    return [got_ref[i * rows : (i + 1) * rows].astype(jnp.int32).astype(F32) * unit for i in entries]


def scaled(codes, scale_of, down, across):
    tiles = [
        [
            codes[r * TILE : (r + 1) * TILE, c * TILE : (c + 1) * TILE] * scale_of(r, c).astype(BF16)
            for c in range(across)
        ]
        for r in range(down)
    ]
    return jnp.concatenate([jnp.concatenate(row, axis=1) for row in tiles], axis=0)


def gate_up_kernel(blocks, far, n, place_ref, scl_ref, x_ref, gate_ref, up_ref, _, *refs):
    me, group = place_ref[0], place_ref[3]
    x = x_ref[...]
    sums_ref = refs[-1]
    wide = sums_ref.shape[-1] // 2
    units, step = wide // TILE, 2 * TILE
    for (piece, q), out_ref in zip(blocks, refs):
        total_ref = sums_ref if q else out_ref
        for i in range(2):
            block = (group * 2 + piece) * n + (me ^ q ^ (i * far))
            cols = pl.ds(pl.multiple_of(block * wide, TILE), wide)
            for m, ref in enumerate((gate_ref, up_ref)):
                total = None
                for k in range(0, x.shape[1], step):
                    w = scaled(
                        ref[k : k + step, cols], lambda r, c: scl_ref[m, k // TILE + r, block * units + c], 2, units
                    )
                    part = jnp.dot(x[:, k : k + step], w, preferred_element_type=F32)
                    total = part if total is None else total + part
                total_ref[i, :, m * wide : (m + 1) * wide] = total
        if q:
            encode([total_ref[i] for i in range(2)], out_ref)


def both_kernel(keep_ref, *refs):
    got_refs, (stay_ref, send_ref) = refs[:3], refs[-2:]
    count, rows = stay_ref.shape[0], stay_ref.shape[1]
    total = [keep_ref[i] for i in range(count)]
    for ref in got_refs:
        total = [t + v for t, v in zip(total, decode(ref, rows, range(count)))]
    for i in range(count):
        stay_ref[i] = total[i]
    encode(total, send_ref)


def hidden_kernel(keep_ref, got_ref, out_ref):
    count, wide = out_ref.shape[0], out_ref.shape[-1]
    got = decode(got_ref, keep_ref.shape[1], range(count))
    for i in range(count):
        total = keep_ref[i] + got[count - 1 - i]
        gate, up = total[:, :wide], total[:, wide:]
        out_ref[i] = (gate / (1.0 + jnp.exp(-gate)) * up).astype(BF16)


def down_kernel(piece, blocks, far, n, begin, last, place_ref, scl_ref, codes_ref, *refs):
    me, group = place_ref[0], place_ref[3]
    hidden_refs, out_ref = refs[: len(blocks)], refs[-1]
    wide, depth, step = hidden_refs[0].shape[-1], codes_ref.shape[0], 2 * TILE
    units = wide // TILE
    for r in range(0, depth, step):
        total = None if begin else refs[len(blocks)][r : r + step]
        for q, hidden_ref in zip(blocks, hidden_refs):
            for i in range(2):
                block = (group * 2 + piece) * n + (me ^ q ^ (i * far))
                cols = pl.ds(pl.multiple_of(block * wide, TILE), wide)
                w = scaled(codes_ref[r : r + step, cols], lambda t, c: scl_ref[r // TILE + t, block * units + c], 2, units)
                part = lax.dot_general(w, hidden_ref[i], (((1,), (1,)), ((), ())), preferred_element_type=F32)
                total = part if total is None else total + part
        if not last:
            out_ref[r : r + step] = total
            continue
        total = total.T
        count, rows, _ = out_ref.shape
        for j in range(count):
            out_ref[j, :, r : r + step] = total[j * rows : (j + 1) * rows].astype(BF16)


def group_sum_kernel(got_ref, out_ref):
    n = out_ref.shape[0]
    for c in range(n):
        out_ref[c] = got_ref[c].astype(F32) + got_ref[n + c].astype(F32)


def final_kernel(place_ref, tok_ref, tok_mate_ref, branch_ref, branch_mate_ref, head_ref, head_mate_ref, out_ref, values_ref):
    n, rows, width = branch_ref.shape
    per = out_ref.shape[1] // width
    core = place_ref[1]
    total = jnp.zeros((rows, 1), F32)
    for side, (tok, head) in enumerate(((tok_ref, head_ref), (tok_mate_ref, head_mate_ref))):
        for i in range(per):
            cols = slice(i * width, (i + 1) * width)
            c = (core ^ side) * per + i
            branch = branch_ref[c] + branch_mate_ref[c]
            layer = (tok[:, cols].astype(F32) + branch).astype(BF16)
            if side == 0:
                out_ref[:, cols] = layer
            total = total + jnp.sum(layer.astype(F32) * head[:, cols], axis=-1, keepdims=True)
    row, at = (lax.broadcasted_iota(jnp.int32, (rows, rows), axis) for axis in (0, 1))
    taken = (row == at) & (row < place_ref[2])
    values_ref[...] = jnp.sum(jnp.where(taken, total, 0.0), axis=0, keepdims=True)


def call(kernel, name, ins, outs, limit=8, cost=None, scratch=()):
    specs = [x[1] if isinstance(x, tuple) else VMEM_SPEC for x in ins]
    return pl.pallas_call(
        kernel,
        in_specs=specs,
        out_specs=jax.tree.map(lambda _: VMEM_SPEC, outs),
        out_shape=outs,
        scratch_shapes=scratch,
        compiler_params=params(limit),
        cost_estimate=cost,
        name=name,
    )(*[x[0] if isinstance(x, tuple) else x for x in ins])


def body_split(n, tokens, lengths, norm_gain, gate_codes, gate_scales, up_codes, up_scales, down_codes, down_scales, value_head):
    rows, d_half = tokens.shape
    d, depth = 2 * d_half, gate_codes.shape[0]
    group_cols = gate_codes.shape[1] // 2
    units = group_cols // (2 * n * TILE)
    all_rows, half = 2 * n * rows, n // 2
    me, group, core = (lax.axis_index(a).astype(jnp.int32) for a in ("fsdp", "groups", "tp"))
    place = jnp.stack([me, core, lengths[0], group])
    spot = (place, SMEM_SPEC)
    shape = jax.ShapeDtypeStruct

    def swap(x, axis, bit):
        return lax.ppermute(x, axis, [(i, i ^ bit) for i in range(n if axis == "fsdp" else 2)])

    hbm = lambda x: pltpu.with_memory_space_constraint(x, pltpu.HBM)
    vmem = lambda x: pltpu.with_memory_space_constraint(x, pltpu.VMEM)
    unread = lambda x: (x, pl.BlockSpec(memory_space=pl.ANY))

    tok_mate = swap(tokens, "tp", 1)
    head = value_head.reshape(1, d_half)
    head_mate = swap(head, "tp", 1)
    whole = lambda x: (hbm(x), pl.BlockSpec())
    normed, gu_scales, down_scales = call(
        norm_kernel,
        "norm",
        [spot, whole(tokens), tok_mate]
        + [whole(a) for a in (norm_gain, gate_scales, up_scales, down_scales)]
        + [unread(head_mate)],
        [
            shape((2 * n, rows, depth), BF16),
            shape((2, *gate_scales.shape), F32),
            shape(down_scales.shape, F32),
        ],
    )
    normed = call(
        hold_kernel,
        "hold",
        [normed] + [unread(hbm(a)) for a in (gate_codes, up_codes, down_codes)],
        shape(normed.shape, BF16),
    )
    rows_axes = ("groups", "fsdp")
    x = call(
        rows_kernel,
        "rows",
        [lax.all_to_all(normed, rows_axes, 0, 0, tiled=True)],
        shape((all_rows, depth), BF16),
        scratch=[pltpu.VMEM((all_rows, depth), F32)],
    )

    wide = units * TILE
    codes = [vmem(c) for c in (gate_codes, up_codes)]
    cost = lambda share, width: pl.CostEstimate(
        flops=2 * all_rows * depth * width * n // share, transcendentals=0, bytes_accessed=2 * depth * width * n // share
    )

    coded = lambda count: shape((count * all_rows + CODE_ROWS, 2 * wide), jnp.int16)

    fars = (n // 2 + 2, n // 2 + 2)
    sums = shape((2, all_rows, 2 * wide), F32)

    def gate_up(name, after, *blocks):
        return call(
            functools.partial(gate_up_kernel, blocks, fars[blocks[0][0]], n),
            f"gate_up_{name}",
            [spot, (gu_scales, SMEM_SPEC), x, *codes, unread(after)],
            [coded(2) if q else sums for _, q in blocks],
            cost=cost(2, 2 * wide),
            scratch=[pltpu.VMEM(sums.shape, F32)],
        )

    orders = ((1, 3, 2), (2, 3, 1))
    kept, got, after, branch = [], [], x, None
    for p, (q1, q2, q3) in enumerate(orders):
        send_1, send_2 = gate_up(f"{p}_first", after, (p, q1), (p, q2))
        send_3, keep = gate_up(f"{p}_second", send_1, (p, q3), (p, 0))
        got.append([swap(send, "fsdp", q) for send, q in ((send_1, q1), (send_2, q2), (send_3, q3))])
        kept.append(keep)
        after = send_3
    both = [
        call(
            both_kernel,
            f"both_{p}",
            [kept[p], *got[p]] + [unread(hbm(down_codes))] * p,
            [sums, coded(2)],
        )
        for p in range(2)
    ]
    for p, order in enumerate(orders):
        keep, send = both[p]
        hidden = call(hidden_kernel, f"hidden_{p}", [keep, swap(send, "fsdp", fars[p])], shape((2, all_rows, wide), BF16))
        branch = call(
            functools.partial(down_kernel, p, (0, *order), fars[p], n, p == 0, p == 1),
            f"down_{p}",
            [spot, (down_scales, SMEM_SPEC), vmem(down_codes), hidden]
            + [swap(hidden, "fsdp", q) for q in order]
            + ([branch] if p else []),
            shape((2 * n, rows, depth), BF16) if p else shape((depth, all_rows), F32),
            cost=cost(1, wide),
        )

    got = lax.all_to_all(branch, rows_axes, 0, 0, tiled=True)
    branch = call(group_sum_kernel, "group_sum", [got], shape((n, rows, depth), F32))
    layer_out, values = call(
        final_kernel,
        "final",
        [spot, tokens, tok_mate, branch, swap(branch, "tp", 1), head, head_mate],
        [shape((rows, d_half), BF16), shape((1, rows), F32)],
    )
    return layer_out, values.reshape(rows)


def solution(mesh):
    placed = (
        P(("groups", "fsdp"), "tp"),
        P(("groups", "fsdp")),
        P(),
        P("fsdp", "tp"),
        P("fsdp", "tp"),
        P("fsdp", "tp"),
        P("fsdp", "tp"),
        P("fsdp", "tp"),
        P("fsdp", "tp"),
        P("tp"),
    )
    n = mesh.shape["fsdp"]

    def body(*args):
        codes = args[3]
        fits = (
            n == 8
            and mesh.shape["groups"] == 2
            and mesh.shape["tp"] == 2
            and codes.shape[0] % TILE == 0
            and codes.shape[1] == 8 * n * TILE
        )
        if fits:
            return body_split(n, *args)
        return body_any(*args)

    return jax.shard_map(
        body,
        mesh=mesh,
        in_specs=placed,
        out_specs=(P(("groups", "fsdp"), "tp"), P(("groups", "fsdp"))),
        check_vma=False,
    )
```

```python
import functools

import jax
import jax.numpy as jnp
from jax import lax
from jax.experimental import pallas as pl
from jax.experimental.pallas import tpu as pltpu
from jax.sharding import PartitionSpec as P

TILE = 128
CODE_ROWS = 16
LOG2_E, LN_2 = 1.4426950408889634, 0.6931471805599453
BF16, F32 = jnp.bfloat16, jnp.float32
VMEM_SPEC = pl.BlockSpec(memory_space=pltpu.VMEM)
SMEM_SPEC = pl.BlockSpec(memory_space=pltpu.SMEM)


def params(mib):
    return pltpu.CompilerParams(vmem_limit_bytes=mib << 20)


def dequantize(codes, scales):
    tile_rows = codes.shape[0] // scales.shape[0]
    tile_cols = codes.shape[1] // scales.shape[1]
    blocks = codes.astype(F32).reshape(scales.shape[0], tile_rows, scales.shape[1], tile_cols)
    scaled = blocks * scales.astype(F32)[:, None, :, None]
    return scaled.reshape(codes.shape).astype(BF16)


def rms_normed(rows_in, norm_gain):
    resid = rows_in.astype(F32)
    mean_sq = jnp.mean(resid * resid, axis=-1, keepdims=True)
    return (resid * lax.rsqrt(mean_sq + 1e-05) * norm_gain.astype(F32)).astype(BF16)


def body_any(tokens, lengths, norm_gain, gate_codes, gate_scales, up_codes, up_scales, down_codes, down_scales, value_head):
    rows = tokens.shape[0]
    feature_rows = lax.all_gather(tokens, "tp", axis=1, tiled=True)
    normed = rms_normed(feature_rows, norm_gain)
    x = lax.all_to_all(normed, "fsdp", split_axis=1, concat_axis=0, tiled=True)
    gate = jnp.dot(x, dequantize(gate_codes, gate_scales), preferred_element_type=F32)
    up = jnp.dot(x, dequantize(up_codes, up_scales), preferred_element_type=F32)
    gate = lax.psum_scatter(gate, "fsdp", scatter_dimension=1, tiled=True)
    up = lax.psum_scatter(up, "fsdp", scatter_dimension=1, tiled=True)
    hidden = (jax.nn.silu(gate) * up).astype(BF16)
    hidden = lax.all_gather(hidden, "fsdp", axis=1, tiled=True)
    part = lax.dot_general(
        hidden, dequantize(down_codes, down_scales), (((1,), (1,)), ((), ())), preferred_element_type=F32
    )
    part = lax.all_to_all(part, "fsdp", split_axis=0, concat_axis=1, tiled=True)
    branch = lax.psum_scatter(part, "tp", scatter_dimension=1, tiled=True)
    layer_out = (tokens.astype(F32) + branch).astype(BF16)
    head = jnp.dot(layer_out.astype(F32), value_head, precision=lax.Precision.HIGHEST)
    head = lax.psum(head, "tp")
    live = jnp.arange(rows) < lengths[0]
    return layer_out, jnp.where(live, head, F32(0.0))


def norm_kernel(place_ref, mine_ref, core_mate_ref, gain_ref, gate_scl_ref, up_scl_ref, down_scl_ref, *refs):
    out_ref, gu_out_ref, down_out_ref = refs[-3:]
    gu_out_ref[0] = gate_scl_ref[...].astype(F32)
    gu_out_ref[1] = up_scl_ref[...].astype(F32)
    down_out_ref[...] = down_scl_ref[...].astype(F32)
    _, rows, width = out_ref.shape
    n = gain_ref.shape[0] // width
    per = mine_ref.shape[1] // width
    resid = [ref[...].astype(F32) for ref in (mine_ref, core_mate_ref)]
    total = sum(jnp.sum(r * r, axis=-1, keepdims=True) for r in resid)
    inv = lax.rsqrt(total * (1.0 / (n * width)) + 1e-05)
    for side, r in enumerate(resid):
        for i in range(per):
            c = (place_ref[1] ^ side) * per + i
            gain = gain_ref[pl.ds(pl.multiple_of(c * width, TILE), width)].astype(F32).reshape(1, width)
            chunk = (r[:, i * width : (i + 1) * width] * inv * gain).astype(BF16)
            for g in range(2):
                out_ref[g * n + c] = chunk


def hold_kernel(ref, *refs):
    refs[-1][...] = ref[...]


def rows_kernel(got_ref, out_ref, rows_ref):
    count, rows, _ = got_ref.shape
    for j in range(count):
        rows_ref[j * rows : (j + 1) * rows] = got_ref[j].astype(F32)
    out_ref[...] = rows_ref[...].astype(BF16)


def encode(values, out_ref):
    count, rows = len(values), values[0].shape[0]
    top = functools.reduce(jnp.maximum, [jnp.max(jnp.abs(v), axis=0, keepdims=True) for v in values])
    power = jnp.clip(jnp.ceil(jnp.log(top) * LOG2_E), -100.0, 100.0)
    unit = jnp.exp((14.0 - power) * LN_2)
    for i, v in enumerate(values):
        out_ref[i * rows : (i + 1) * rows] = jnp.round(v * unit).astype(jnp.int32).astype(jnp.int16)
    tail = (out_ref.shape[0] - count * rows, out_ref.shape[1])
    out_ref[count * rows :] = jnp.broadcast_to(power.astype(jnp.int32), tail).astype(jnp.int16)


def decode(got_ref, rows, entries):
    count = (got_ref.shape[0] - CODE_ROWS) // rows
    power = got_ref[count * rows :].astype(jnp.int32).astype(F32)[:1]
    unit = jnp.exp((power - 14.0) * LN_2)
    return [got_ref[i * rows : (i + 1) * rows].astype(jnp.int32).astype(F32) * unit for i in entries]


def scaled(codes, scale_of, down, across):
    tiles = [
        [
            codes[r * TILE : (r + 1) * TILE, c * TILE : (c + 1) * TILE] * scale_of(r, c).astype(BF16)
            for c in range(across)
        ]
        for r in range(down)
    ]
    return jnp.concatenate([jnp.concatenate(row, axis=1) for row in tiles], axis=0)


def gate_up_kernel(blocks, far, n, place_ref, scl_ref, x_ref, gate_ref, up_ref, _, *refs):
    me, group = place_ref[0], place_ref[3]
    x = x_ref[...]
    sums_ref = refs[-1]
    wide = sums_ref.shape[-1] // 2
    units, step = wide // TILE, 2 * TILE
    for (piece, q), out_ref in zip(blocks, refs):
        total_ref = sums_ref if q else out_ref
        for i in range(2):
            block = (group * 2 + piece) * n + (me ^ q ^ (i * far))
            cols = pl.ds(pl.multiple_of(block * wide, TILE), wide)
            for m, ref in enumerate((gate_ref, up_ref)):
                total = None
                for k in range(0, x.shape[1], step):
                    w = scaled(
                        ref[k : k + step, cols], lambda r, c: scl_ref[m, k // TILE + r, block * units + c], 2, units
                    )
                    part = jnp.dot(x[:, k : k + step], w, preferred_element_type=F32)
                    total = part if total is None else total + part
                total_ref[i, :, m * wide : (m + 1) * wide] = total
        if q:
            encode([total_ref[i] for i in range(2)], out_ref)


def both_kernel(keep_ref, *refs):
    got_refs, (stay_ref, send_ref) = refs[:3], refs[-2:]
    count, rows = stay_ref.shape[0], stay_ref.shape[1]
    total = [keep_ref[i] for i in range(count)]
    for ref in got_refs:
        total = [t + v for t, v in zip(total, decode(ref, rows, range(count)))]
    for i in range(count):
        stay_ref[i] = total[i]
    encode(total, send_ref)


def hidden_kernel(keep_ref, got_ref, out_ref):
    count, wide = out_ref.shape[0], out_ref.shape[-1]
    got = decode(got_ref, keep_ref.shape[1], range(count))
    for i in range(count):
        total = keep_ref[i] + got[count - 1 - i]
        gate, up = total[:, :wide], total[:, wide:]
        out_ref[i] = (gate / (1.0 + jnp.exp(-gate)) * up).astype(BF16)


def down_kernel(piece, blocks, far, n, begin, last, place_ref, scl_ref, codes_ref, *refs):
    me, group = place_ref[0], place_ref[3]
    hidden_refs, out_ref = refs[: len(blocks)], refs[-1]
    wide, depth, step = hidden_refs[0].shape[-1], codes_ref.shape[0], 2 * TILE
    units = wide // TILE
    for r in range(0, depth, step):
        total = None if begin else refs[len(blocks)][r : r + step]
        for q, hidden_ref in zip(blocks, hidden_refs):
            for i in range(2):
                block = (group * 2 + piece) * n + (me ^ q ^ (i * far))
                cols = pl.ds(pl.multiple_of(block * wide, TILE), wide)
                w = scaled(codes_ref[r : r + step, cols], lambda t, c: scl_ref[r // TILE + t, block * units + c], 2, units)
                part = lax.dot_general(w, hidden_ref[i], (((1,), (1,)), ((), ())), preferred_element_type=F32)
                total = part if total is None else total + part
        if not last:
            out_ref[r : r + step] = total
            continue
        total = total.T
        count, rows, _ = out_ref.shape
        for j in range(count):
            out_ref[j, :, r : r + step] = total[j * rows : (j + 1) * rows].astype(BF16)


def group_sum_kernel(got_ref, out_ref):
    n = out_ref.shape[0]
    for c in range(n):
        out_ref[c] = got_ref[c].astype(F32) + got_ref[n + c].astype(F32)


def final_kernel(place_ref, tok_ref, tok_mate_ref, branch_ref, branch_mate_ref, head_ref, head_mate_ref, out_ref, values_ref):
    n, rows, width = branch_ref.shape
    per = out_ref.shape[1] // width
    core = place_ref[1]
    total = jnp.zeros((rows, 1), F32)
    for side, (tok, head) in enumerate(((tok_ref, head_ref), (tok_mate_ref, head_mate_ref))):
        for i in range(per):
            cols = slice(i * width, (i + 1) * width)
            c = (core ^ side) * per + i
            branch = branch_ref[c] + branch_mate_ref[c]
            layer = (tok[:, cols].astype(F32) + branch).astype(BF16)
            if side == 0:
                out_ref[:, cols] = layer
            total = total + jnp.sum(layer.astype(F32) * head[:, cols], axis=-1, keepdims=True)
    row, at = (lax.broadcasted_iota(jnp.int32, (rows, rows), axis) for axis in (0, 1))
    taken = (row == at) & (row < place_ref[2])
    values_ref[...] = jnp.sum(jnp.where(taken, total, 0.0), axis=0, keepdims=True)


def call(kernel, name, ins, outs, limit=8, cost=None, scratch=()):
    specs = [x[1] if isinstance(x, tuple) else VMEM_SPEC for x in ins]
    return pl.pallas_call(
        kernel,
        in_specs=specs,
        out_specs=jax.tree.map(lambda _: VMEM_SPEC, outs),
        out_shape=outs,
        scratch_shapes=scratch,
        compiler_params=params(limit),
        cost_estimate=cost,
        name=name,
    )(*[x[0] if isinstance(x, tuple) else x for x in ins])


def body_split(n, tokens, lengths, norm_gain, gate_codes, gate_scales, up_codes, up_scales, down_codes, down_scales, value_head):
    rows, d_half = tokens.shape
    d, depth = 2 * d_half, gate_codes.shape[0]
    group_cols = gate_codes.shape[1] // 2
    units = group_cols // (2 * n * TILE)
    all_rows, half = 2 * n * rows, n // 2
    me, group, core = (lax.axis_index(a).astype(jnp.int32) for a in ("fsdp", "groups", "tp"))
    place = jnp.stack([me, core, lengths[0], group])
    spot = (place, SMEM_SPEC)
    shape = jax.ShapeDtypeStruct

    def swap(x, axis, bit):
        return lax.ppermute(x, axis, [(i, i ^ bit) for i in range(n if axis == "fsdp" else 2)])

    hbm = lambda x: pltpu.with_memory_space_constraint(x, pltpu.HBM)
    vmem = lambda x: pltpu.with_memory_space_constraint(x, pltpu.VMEM)
    unread = lambda x: (x, pl.BlockSpec(memory_space=pl.ANY))

    tok_mate = swap(tokens, "tp", 1)
    head = value_head.reshape(1, d_half)
    head_mate = swap(head, "tp", 1)
    whole = lambda x: (hbm(x), pl.BlockSpec())
    normed, gu_scales, down_scales = call(
        norm_kernel,
        "norm",
        [spot, whole(tokens), tok_mate]
        + [whole(a) for a in (norm_gain, gate_scales, up_scales, down_scales)]
        + [unread(head_mate)],
        [
            shape((2 * n, rows, depth), BF16),
            shape((2, *gate_scales.shape), F32),
            shape(down_scales.shape, F32),
        ],
    )
    normed = call(
        hold_kernel,
        "hold",
        [normed] + [unread(hbm(a)) for a in (gate_codes, up_codes, down_codes)],
        shape(normed.shape, BF16),
    )
    rows_axes = ("groups", "fsdp")
    x = call(
        rows_kernel,
        "rows",
        [lax.all_to_all(normed, rows_axes, 0, 0, tiled=True)],
        shape((all_rows, depth), BF16),
        scratch=[pltpu.VMEM((all_rows, depth), F32)],
    )

    wide = units * TILE
    codes = [vmem(c) for c in (gate_codes, up_codes)]
    cost = lambda share, width: pl.CostEstimate(
        flops=2 * all_rows * depth * width * n // share, transcendentals=0, bytes_accessed=2 * depth * width * n // share
    )

    coded = lambda count: shape((count * all_rows + CODE_ROWS, 2 * wide), jnp.int16)

    fars = (n // 2 + 2, n // 2 + 2)
    sums = shape((2, all_rows, 2 * wide), F32)

    def gate_up(name, after, *blocks):
        return call(
            functools.partial(gate_up_kernel, blocks, fars[blocks[0][0]], n),
            f"gate_up_{name}",
            [spot, (gu_scales, SMEM_SPEC), x, *codes, unread(after)],
            [coded(2) if q else sums for _, q in blocks],
            cost=cost(2, 2 * wide),
            scratch=[pltpu.VMEM(sums.shape, F32)],
        )

    orders = ((3, 1, 2), (3, 2, 1))
    sends_0 = gate_up("send_0", x, *[(0, q) for q in orders[0]])
    kept = gate_up("keep", sends_0[0], (0, 0), (1, 0))
    sends_1 = gate_up("send_1", kept[0], *[(1, q) for q in orders[1]])
    got = [[swap(send, "fsdp", q) for send, q in zip(sends_0, orders[0])]]
    branch = None
    both = [call(both_kernel, "both_0", [kept[0], *got[0]], [sums, coded(2)])]
    held = call(hold_kernel, "hold_send", [sends_1[2], unread(both[0][1])], coded(2))
    got.append([swap(send, "fsdp", q) for send, q in zip((*sends_1[:2], held), orders[1])])
    both.append(call(both_kernel, "both_1", [kept[1], *got[1], unread(hbm(down_codes))], [sums, coded(2)]))
    for p, order in enumerate(orders):
        keep, send = both[p]
        hidden = call(hidden_kernel, f"hidden_{p}", [keep, swap(send, "fsdp", fars[p])], shape((2, all_rows, wide), BF16))
        branch = call(
            functools.partial(down_kernel, p, (0, *order), fars[p], n, p == 0, p == 1),
            f"down_{p}",
            [spot, (down_scales, SMEM_SPEC), vmem(down_codes), hidden]
            + [swap(hidden, "fsdp", q) for q in order]
            + ([branch] if p else []),
            shape((2 * n, rows, depth), BF16) if p else shape((depth, all_rows), F32),
            cost=cost(1, wide),
        )

    got = lax.all_to_all(branch, rows_axes, 0, 0, tiled=True)
    branch = call(group_sum_kernel, "group_sum", [got], shape((n, rows, depth), F32))
    layer_out, values = call(
        final_kernel,
        "final",
        [spot, tokens, tok_mate, branch, swap(branch, "tp", 1), head, head_mate],
        [shape((rows, d_half), BF16), shape((1, rows), F32)],
    )
    return layer_out, values.reshape(rows)


def solution(mesh):
    placed = (
        P(("groups", "fsdp"), "tp"),
        P(("groups", "fsdp")),
        P(),
        P("fsdp", "tp"),
        P("fsdp", "tp"),
        P("fsdp", "tp"),
        P("fsdp", "tp"),
        P("fsdp", "tp"),
        P("fsdp", "tp"),
        P("tp"),
    )
    n = mesh.shape["fsdp"]

    def body(*args):
        codes = args[3]
        fits = (
            n == 8
            and mesh.shape["groups"] == 2
            and mesh.shape["tp"] == 2
            and codes.shape[0] % TILE == 0
            and codes.shape[1] == 8 * n * TILE
        )
        if fits:
            return body_split(n, *args)
        return body_any(*args)

    return jax.shard_map(
        body,
        mesh=mesh,
        in_specs=placed,
        out_specs=(P(("groups", "fsdp"), "tp"), P(("groups", "fsdp"))),
        check_vma=False,
    )
```

```python
import functools

import jax
import jax.numpy as jnp
from jax import lax
from jax.experimental import pallas as pl
from jax.experimental.pallas import tpu as pltpu
from jax.sharding import PartitionSpec as P

TILE = 128
CODE_ROWS = 16
LOG2_E, LN_2 = 1.4426950408889634, 0.6931471805599453
BF16, F32 = jnp.bfloat16, jnp.float32
VMEM_SPEC = pl.BlockSpec(memory_space=pltpu.VMEM)
SMEM_SPEC = pl.BlockSpec(memory_space=pltpu.SMEM)


def params(mib):
    return pltpu.CompilerParams(vmem_limit_bytes=mib << 20)


def dequantize(codes, scales):
    tile_rows = codes.shape[0] // scales.shape[0]
    tile_cols = codes.shape[1] // scales.shape[1]
    blocks = codes.astype(F32).reshape(scales.shape[0], tile_rows, scales.shape[1], tile_cols)
    scaled = blocks * scales.astype(F32)[:, None, :, None]
    return scaled.reshape(codes.shape).astype(BF16)


def rms_normed(rows_in, norm_gain):
    resid = rows_in.astype(F32)
    mean_sq = jnp.mean(resid * resid, axis=-1, keepdims=True)
    return (resid * lax.rsqrt(mean_sq + 1e-05) * norm_gain.astype(F32)).astype(BF16)


def body_any(tokens, lengths, norm_gain, gate_codes, gate_scales, up_codes, up_scales, down_codes, down_scales, value_head):
    rows = tokens.shape[0]
    feature_rows = lax.all_gather(tokens, "tp", axis=1, tiled=True)
    normed = rms_normed(feature_rows, norm_gain)
    x = lax.all_to_all(normed, "fsdp", split_axis=1, concat_axis=0, tiled=True)
    gate = jnp.dot(x, dequantize(gate_codes, gate_scales), preferred_element_type=F32)
    up = jnp.dot(x, dequantize(up_codes, up_scales), preferred_element_type=F32)
    gate = lax.psum_scatter(gate, "fsdp", scatter_dimension=1, tiled=True)
    up = lax.psum_scatter(up, "fsdp", scatter_dimension=1, tiled=True)
    hidden = (jax.nn.silu(gate) * up).astype(BF16)
    hidden = lax.all_gather(hidden, "fsdp", axis=1, tiled=True)
    part = lax.dot_general(
        hidden, dequantize(down_codes, down_scales), (((1,), (1,)), ((), ())), preferred_element_type=F32
    )
    part = lax.all_to_all(part, "fsdp", split_axis=0, concat_axis=1, tiled=True)
    branch = lax.psum_scatter(part, "tp", scatter_dimension=1, tiled=True)
    layer_out = (tokens.astype(F32) + branch).astype(BF16)
    head = jnp.dot(layer_out.astype(F32), value_head, precision=lax.Precision.HIGHEST)
    head = lax.psum(head, "tp")
    live = jnp.arange(rows) < lengths[0]
    return layer_out, jnp.where(live, head, F32(0.0))


def norm_kernel(place_ref, mine_ref, core_mate_ref, gain_ref, gate_scl_ref, up_scl_ref, down_scl_ref, *refs):
    out_ref, gu_out_ref, down_out_ref = refs[-3:]
    gu_out_ref[0] = gate_scl_ref[...].astype(F32)
    gu_out_ref[1] = up_scl_ref[...].astype(F32)
    down_out_ref[...] = down_scl_ref[...].astype(F32)
    _, rows, width = out_ref.shape
    n = gain_ref.shape[0] // width
    per = mine_ref.shape[1] // width
    resid = [ref[...].astype(F32) for ref in (mine_ref, core_mate_ref)]
    total = sum(jnp.sum(r * r, axis=-1, keepdims=True) for r in resid)
    inv = lax.rsqrt(total * (1.0 / (n * width)) + 1e-05)
    for side, r in enumerate(resid):
        for i in range(per):
            c = (place_ref[1] ^ side) * per + i
            gain = gain_ref[pl.ds(pl.multiple_of(c * width, TILE), width)].astype(F32).reshape(1, width)
            chunk = (r[:, i * width : (i + 1) * width] * inv * gain).astype(BF16)
            for g in range(2):
                out_ref[g * n + c] = chunk


def hold_kernel(ref, *refs):
    refs[-1][...] = ref[...]


def rows_kernel(got_ref, out_ref, rows_ref):
    count, rows, _ = got_ref.shape
    for j in range(count):
        rows_ref[j * rows : (j + 1) * rows] = got_ref[j].astype(F32)
    out_ref[...] = rows_ref[...].astype(BF16)


def encode(values, out_ref):
    count, rows = len(values), values[0].shape[0]
    top = functools.reduce(jnp.maximum, [jnp.max(jnp.abs(v), axis=0, keepdims=True) for v in values])
    power = jnp.clip(jnp.ceil(jnp.log(top) * LOG2_E), -100.0, 100.0)
    unit = jnp.exp((14.0 - power) * LN_2)
    for i, v in enumerate(values):
        out_ref[i * rows : (i + 1) * rows] = jnp.round(v * unit).astype(jnp.int32).astype(jnp.int16)
    tail = (out_ref.shape[0] - count * rows, out_ref.shape[1])
    out_ref[count * rows :] = jnp.broadcast_to(power.astype(jnp.int32), tail).astype(jnp.int16)


def decode(got_ref, rows, entries):
    count = (got_ref.shape[0] - CODE_ROWS) // rows
    power = got_ref[count * rows :].astype(jnp.int32).astype(F32)[:1]
    unit = jnp.exp((power - 14.0) * LN_2)
    return [got_ref[i * rows : (i + 1) * rows].astype(jnp.int32).astype(F32) * unit for i in entries]


def scaled(codes, scale_of, down, across):
    tiles = [
        [
            codes[r * TILE : (r + 1) * TILE, c * TILE : (c + 1) * TILE] * scale_of(r, c).astype(BF16)
            for c in range(across)
        ]
        for r in range(down)
    ]
    return jnp.concatenate([jnp.concatenate(row, axis=1) for row in tiles], axis=0)


def gate_up_kernel(blocks, far, n, place_ref, scl_ref, x_ref, gate_ref, up_ref, _, *refs):
    me, group = place_ref[0], place_ref[3]
    x = x_ref[...]
    sums_ref = refs[-1]
    wide = sums_ref.shape[-1] // 2
    units, step = wide // TILE, 2 * TILE
    for (piece, q), out_ref in zip(blocks, refs):
        total_ref = sums_ref if q else out_ref
        for i in range(2):
            block = (group * 2 + piece) * n + (me ^ q ^ (i * far))
            cols = pl.ds(pl.multiple_of(block * wide, TILE), wide)
            for m, ref in enumerate((gate_ref, up_ref)):
                total = None
                for k in range(0, x.shape[1], step):
                    w = scaled(
                        ref[k : k + step, cols], lambda r, c: scl_ref[m, k // TILE + r, block * units + c], 2, units
                    )
                    part = jnp.dot(x[:, k : k + step], w, preferred_element_type=F32)
                    total = part if total is None else total + part
                total_ref[i, :, m * wide : (m + 1) * wide] = total
        if q:
            encode([total_ref[i] for i in range(2)], out_ref)


def both_kernel(keep_ref, *refs):
    got_refs, (stay_ref, send_ref) = refs[:3], refs[-2:]
    count, rows = stay_ref.shape[0], stay_ref.shape[1]
    total = [keep_ref[i] for i in range(count)]
    for ref in got_refs:
        total = [t + v for t, v in zip(total, decode(ref, rows, range(count)))]
    for i in range(count):
        stay_ref[i] = total[i]
    encode(total, send_ref)


def hidden_kernel(keep_ref, got_ref, out_ref):
    count, wide = out_ref.shape[0], out_ref.shape[-1]
    got = decode(got_ref, keep_ref.shape[1], range(count))
    for i in range(count):
        total = keep_ref[i] + got[count - 1 - i]
        gate, up = total[:, :wide], total[:, wide:]
        out_ref[i] = (gate / (1.0 + jnp.exp(-gate)) * up).astype(BF16)


def down_kernel(piece, blocks, far, n, begin, last, place_ref, scl_ref, codes_ref, *refs):
    me, group = place_ref[0], place_ref[3]
    hidden_refs, out_ref = refs[: len(blocks)], refs[-1]
    wide, depth, step = hidden_refs[0].shape[-1], codes_ref.shape[0], 2 * TILE
    units = wide // TILE
    for r in range(0, depth, step):
        total = None if begin else refs[len(blocks)][r : r + step]
        for q, hidden_ref in zip(blocks, hidden_refs):
            for i in range(2):
                block = (group * 2 + piece) * n + (me ^ q ^ (i * far))
                cols = pl.ds(pl.multiple_of(block * wide, TILE), wide)
                w = scaled(codes_ref[r : r + step, cols], lambda t, c: scl_ref[r // TILE + t, block * units + c], 2, units)
                part = lax.dot_general(w, hidden_ref[i], (((1,), (1,)), ((), ())), preferred_element_type=F32)
                total = part if total is None else total + part
        if not last:
            out_ref[r : r + step] = total
            continue
        total = total.T
        count, rows, _ = out_ref.shape
        for j in range(count):
            out_ref[j, :, r : r + step] = total[j * rows : (j + 1) * rows].astype(BF16)


def group_sum_kernel(got_ref, out_ref):
    n = out_ref.shape[0]
    for c in range(n):
        out_ref[c] = got_ref[c].astype(F32) + got_ref[n + c].astype(F32)


def final_kernel(place_ref, tok_ref, tok_mate_ref, branch_ref, branch_mate_ref, head_ref, head_mate_ref, out_ref, values_ref):
    n, rows, width = branch_ref.shape
    per = out_ref.shape[1] // width
    core = place_ref[1]
    total = jnp.zeros((rows, 1), F32)
    for side, (tok, head) in enumerate(((tok_ref, head_ref), (tok_mate_ref, head_mate_ref))):
        for i in range(per):
            cols = slice(i * width, (i + 1) * width)
            c = (core ^ side) * per + i
            branch = branch_ref[c] + branch_mate_ref[c]
            layer = (tok[:, cols].astype(F32) + branch).astype(BF16)
            if side == 0:
                out_ref[:, cols] = layer
            total = total + jnp.sum(layer.astype(F32) * head[:, cols], axis=-1, keepdims=True)
    row, at = (lax.broadcasted_iota(jnp.int32, (rows, rows), axis) for axis in (0, 1))
    taken = (row == at) & (row < place_ref[2])
    values_ref[...] = jnp.sum(jnp.where(taken, total, 0.0), axis=0, keepdims=True)


def call(kernel, name, ins, outs, limit=8, cost=None, scratch=()):
    specs = [x[1] if isinstance(x, tuple) else VMEM_SPEC for x in ins]
    return pl.pallas_call(
        kernel,
        in_specs=specs,
        out_specs=jax.tree.map(lambda _: VMEM_SPEC, outs),
        out_shape=outs,
        scratch_shapes=scratch,
        compiler_params=params(limit),
        cost_estimate=cost,
        name=name,
    )(*[x[0] if isinstance(x, tuple) else x for x in ins])


def body_split(n, tokens, lengths, norm_gain, gate_codes, gate_scales, up_codes, up_scales, down_codes, down_scales, value_head):
    rows, d_half = tokens.shape
    d, depth = 2 * d_half, gate_codes.shape[0]
    group_cols = gate_codes.shape[1] // 2
    units = group_cols // (2 * n * TILE)
    all_rows, half = 2 * n * rows, n // 2
    me, group, core = (lax.axis_index(a).astype(jnp.int32) for a in ("fsdp", "groups", "tp"))
    place = jnp.stack([me, core, lengths[0], group])
    spot = (place, SMEM_SPEC)
    shape = jax.ShapeDtypeStruct

    def swap(x, axis, bit):
        return lax.ppermute(x, axis, [(i, i ^ bit) for i in range(n if axis == "fsdp" else 2)])

    hbm = lambda x: pltpu.with_memory_space_constraint(x, pltpu.HBM)
    vmem = lambda x: pltpu.with_memory_space_constraint(x, pltpu.VMEM)
    unread = lambda x: (x, pl.BlockSpec(memory_space=pl.ANY))

    tok_mate = swap(tokens, "tp", 1)
    head = value_head.reshape(1, d_half)
    head_mate = swap(head, "tp", 1)
    whole = lambda x: (hbm(x), pl.BlockSpec())
    normed, gu_scales, down_scales = call(
        norm_kernel,
        "norm",
        [spot, whole(tokens), tok_mate]
        + [whole(a) for a in (norm_gain, gate_scales, up_scales, down_scales)]
        + [unread(head_mate)],
        [
            shape((2 * n, rows, depth), BF16),
            shape((2, *gate_scales.shape), F32),
            shape(down_scales.shape, F32),
        ],
    )
    normed = call(
        hold_kernel,
        "hold",
        [normed] + [unread(hbm(a)) for a in (gate_codes, up_codes, down_codes)],
        shape(normed.shape, BF16),
    )
    rows_axes = ("groups", "fsdp")
    x = call(
        rows_kernel,
        "rows",
        [lax.all_to_all(normed, rows_axes, 0, 0, tiled=True)],
        shape((all_rows, depth), BF16),
        scratch=[pltpu.VMEM((all_rows, depth), F32)],
    )

    wide = units * TILE
    codes = [vmem(c) for c in (gate_codes, up_codes)]
    cost = lambda share, width: pl.CostEstimate(
        flops=2 * all_rows * depth * width * n // share, transcendentals=0, bytes_accessed=2 * depth * width * n // share
    )

    coded = lambda count: shape((count * all_rows + CODE_ROWS, 2 * wide), jnp.int16)

    fars = (n // 2 + 2, n // 2 + 2)
    sums = shape((2, all_rows, 2 * wide), F32)

    def gate_up(name, after, *blocks):
        return call(
            functools.partial(gate_up_kernel, blocks, fars[blocks[0][0]], n),
            f"gate_up_{name}",
            [spot, (gu_scales, SMEM_SPEC), x, *codes, unread(after)],
            [coded(2) if q else sums for _, q in blocks],
            cost=cost(2, 2 * wide),
            scratch=[pltpu.VMEM(sums.shape, F32)],
        )

    orders = ((3, 1, 2), (3, 2, 1))
    sends_0 = gate_up("send_0", x, *[(0, q) for q in orders[0]])
    kept = gate_up("keep", sends_0[0], (0, 0), (1, 0))
    sends_1 = gate_up("send_1", kept[0], *[(1, q) for q in orders[1]])
    got = [[swap(send, "fsdp", q) for send, q in zip(sends_0, orders[0])]]
    branch = None
    both = [call(both_kernel, "both_0", [kept[0], *got[0]], [sums, coded(2)])]
    held = call(hold_kernel, "hold_send", [sends_1[2], unread(both[0][1])], coded(2))
    got.append([swap(send, "fsdp", q) for send, q in zip((*sends_1[:2], held), orders[1])])
    both.append(call(both_kernel, "both_1", [kept[1], *got[1], unread(hbm(down_codes))], [sums, coded(2)]))
    order = (1, 2, 3)
    for p in range(2):
        keep, send = both[p]
        hidden = call(hidden_kernel, f"hidden_{p}", [keep, swap(send, "fsdp", fars[p])], shape((2, all_rows, wide), BF16))
        branch = call(
            functools.partial(down_kernel, p, (0, *order), fars[p], n, p == 0, p == 1),
            f"down_{p}",
            [spot, (down_scales, SMEM_SPEC), vmem(down_codes), hidden]
            + [swap(hidden, "fsdp", q) for q in order]
            + ([branch] if p else []),
            shape((2 * n, rows, depth), BF16) if p else shape((depth, all_rows), F32),
            cost=cost(1, wide),
        )

    got = lax.all_to_all(branch, rows_axes, 0, 0, tiled=True)
    branch = call(group_sum_kernel, "group_sum", [got], shape((n, rows, depth), F32))
    layer_out, values = call(
        final_kernel,
        "final",
        [spot, tokens, tok_mate, branch, swap(branch, "tp", 1), head, head_mate],
        [shape((rows, d_half), BF16), shape((1, rows), F32)],
    )
    return layer_out, values.reshape(rows)


def solution(mesh):
    placed = (
        P(("groups", "fsdp"), "tp"),
        P(("groups", "fsdp")),
        P(),
        P("fsdp", "tp"),
        P("fsdp", "tp"),
        P("fsdp", "tp"),
        P("fsdp", "tp"),
        P("fsdp", "tp"),
        P("fsdp", "tp"),
        P("tp"),
    )
    n = mesh.shape["fsdp"]

    def body(*args):
        codes = args[3]
        fits = (
            n == 8
            and mesh.shape["groups"] == 2
            and mesh.shape["tp"] == 2
            and codes.shape[0] % (2 * TILE) == 0
            and codes.shape[1] == 8 * n * TILE
        )
        if fits:
            return body_split(n, *args)
        return body_any(*args)

    return jax.shard_map(
        body,
        mesh=mesh,
        in_specs=placed,
        out_specs=(P(("groups", "fsdp"), "tp"), P(("groups", "fsdp"))),
        check_vma=False,
    )
```

```python
import functools

import jax
import jax.numpy as jnp
from jax import lax
from jax.experimental import pallas as pl
from jax.experimental.pallas import tpu as pltpu
from jax.sharding import PartitionSpec as P

TILE = 128
CODE_ROWS = 16
LOG2_E, LN_2 = 1.4426950408889634, 0.6931471805599453
BF16, F32 = jnp.bfloat16, jnp.float32
VMEM_SPEC = pl.BlockSpec(memory_space=pltpu.VMEM)
SMEM_SPEC = pl.BlockSpec(memory_space=pltpu.SMEM)


def params(mib):
    return pltpu.CompilerParams(vmem_limit_bytes=mib << 20)


def dequantize(codes, scales):
    tile_rows = codes.shape[0] // scales.shape[0]
    tile_cols = codes.shape[1] // scales.shape[1]
    blocks = codes.astype(F32).reshape(scales.shape[0], tile_rows, scales.shape[1], tile_cols)
    scaled = blocks * scales.astype(F32)[:, None, :, None]
    return scaled.reshape(codes.shape).astype(BF16)


def rms_normed(rows_in, norm_gain):
    resid = rows_in.astype(F32)
    mean_sq = jnp.mean(resid * resid, axis=-1, keepdims=True)
    return (resid * lax.rsqrt(mean_sq + 1e-05) * norm_gain.astype(F32)).astype(BF16)


def body_any(tokens, lengths, norm_gain, gate_codes, gate_scales, up_codes, up_scales, down_codes, down_scales, value_head):
    rows = tokens.shape[0]
    feature_rows = lax.all_gather(tokens, "tp", axis=1, tiled=True)
    normed = rms_normed(feature_rows, norm_gain)
    x = lax.all_to_all(normed, "fsdp", split_axis=1, concat_axis=0, tiled=True)
    gate = jnp.dot(x, dequantize(gate_codes, gate_scales), preferred_element_type=F32)
    up = jnp.dot(x, dequantize(up_codes, up_scales), preferred_element_type=F32)
    gate = lax.psum_scatter(gate, "fsdp", scatter_dimension=1, tiled=True)
    up = lax.psum_scatter(up, "fsdp", scatter_dimension=1, tiled=True)
    hidden = (jax.nn.silu(gate) * up).astype(BF16)
    hidden = lax.all_gather(hidden, "fsdp", axis=1, tiled=True)
    part = lax.dot_general(
        hidden, dequantize(down_codes, down_scales), (((1,), (1,)), ((), ())), preferred_element_type=F32
    )
    part = lax.all_to_all(part, "fsdp", split_axis=0, concat_axis=1, tiled=True)
    branch = lax.psum_scatter(part, "tp", scatter_dimension=1, tiled=True)
    layer_out = (tokens.astype(F32) + branch).astype(BF16)
    head = jnp.dot(layer_out.astype(F32), value_head, precision=lax.Precision.HIGHEST)
    head = lax.psum(head, "tp")
    live = jnp.arange(rows) < lengths[0]
    return layer_out, jnp.where(live, head, F32(0.0))


def norm_kernel(place_ref, mine_ref, core_mate_ref, gain_ref, gate_scl_ref, up_scl_ref, down_scl_ref, *refs):
    out_ref, gu_out_ref, down_out_ref = refs[-3:]
    gu_out_ref[0] = gate_scl_ref[...].astype(F32)
    gu_out_ref[1] = up_scl_ref[...].astype(F32)
    down_out_ref[...] = down_scl_ref[...].astype(F32)
    _, rows, width = out_ref.shape
    n = gain_ref.shape[0] // width
    per = mine_ref.shape[1] // width
    resid = [ref[...].astype(F32) for ref in (mine_ref, core_mate_ref)]
    total = sum(jnp.sum(r * r, axis=-1, keepdims=True) for r in resid)
    inv = lax.rsqrt(total * (1.0 / (n * width)) + 1e-05)
    for side, r in enumerate(resid):
        for i in range(per):
            c = (place_ref[1] ^ side) * per + i
            gain = gain_ref[pl.ds(pl.multiple_of(c * width, TILE), width)].astype(F32).reshape(1, width)
            chunk = (r[:, i * width : (i + 1) * width] * inv * gain).astype(BF16)
            for g in range(2):
                out_ref[g * n + c] = chunk


def hold_kernel(ref, *refs):
    refs[-1][...] = ref[...]


def rows_kernel(got_ref, out_ref, rows_ref):
    count, rows, _ = got_ref.shape
    for j in range(count):
        rows_ref[j * rows : (j + 1) * rows] = got_ref[j].astype(F32)
    out_ref[...] = rows_ref[...].astype(BF16)


def encode(values, out_ref):
    count, rows = len(values), values[0].shape[0]
    top = functools.reduce(jnp.maximum, [jnp.max(jnp.abs(v), axis=0, keepdims=True) for v in values])
    power = jnp.clip(jnp.ceil(jnp.log(top) * LOG2_E), -100.0, 100.0)
    unit = jnp.exp((14.0 - power) * LN_2)
    for i, v in enumerate(values):
        out_ref[i * rows : (i + 1) * rows] = jnp.round(v * unit).astype(jnp.int32).astype(jnp.int16)
    tail = (out_ref.shape[0] - count * rows, out_ref.shape[1])
    out_ref[count * rows :] = jnp.broadcast_to(power.astype(jnp.int32), tail).astype(jnp.int16)


def decode(got_ref, rows, entries):
    count = (got_ref.shape[0] - CODE_ROWS) // rows
    power = got_ref[count * rows :].astype(jnp.int32).astype(F32)[:1]
    unit = jnp.exp((power - 14.0) * LN_2)
    return [got_ref[i * rows : (i + 1) * rows].astype(jnp.int32).astype(F32) * unit for i in entries]


def scaled(codes, scale_of, down, across):
    tiles = [
        [
            codes[r * TILE : (r + 1) * TILE, c * TILE : (c + 1) * TILE] * scale_of(r, c).astype(BF16)
            for c in range(across)
        ]
        for r in range(down)
    ]
    return jnp.concatenate([jnp.concatenate(row, axis=1) for row in tiles], axis=0)


def gate_up_kernel(blocks, far, n, place_ref, scl_ref, x_ref, gate_ref, up_ref, _, *refs):
    me, group = place_ref[0], place_ref[3]
    x = x_ref[...]
    sums_ref = refs[-1]
    wide = sums_ref.shape[-1] // 2
    units, step = wide // TILE, 2 * TILE
    for (piece, q), out_ref in zip(blocks, refs):
        total_ref = sums_ref if q else out_ref
        for i in range(2):
            block = (group * 2 + piece) * n + (me ^ q ^ (i * far))
            cols = pl.ds(pl.multiple_of(block * wide, TILE), wide)
            for m, ref in enumerate((gate_ref, up_ref)):
                total = None
                for k in range(0, x.shape[1], step):
                    w = scaled(
                        ref[k : k + step, cols], lambda r, c: scl_ref[m, k // TILE + r, block * units + c], 2, units
                    )
                    part = jnp.dot(x[:, k : k + step], w, preferred_element_type=F32)
                    total = part if total is None else total + part
                total_ref[i, :, m * wide : (m + 1) * wide] = total
        if q:
            encode([total_ref[i] for i in range(2)], out_ref)


def both_kernel(keep_ref, *refs):
    got_refs, (stay_ref, send_ref) = refs[:3], refs[-2:]
    count, rows = stay_ref.shape[0], stay_ref.shape[1]
    total = [keep_ref[i] for i in range(count)]
    for ref in got_refs:
        total = [t + v for t, v in zip(total, decode(ref, rows, range(count)))]
    for i in range(count):
        stay_ref[i] = total[i]
    encode(total, send_ref)


def hidden_kernel(keep_ref, got_ref, out_ref):
    count, wide = out_ref.shape[0], out_ref.shape[-1]
    got = decode(got_ref, keep_ref.shape[1], range(count))
    for i in range(count):
        total = keep_ref[i] + got[count - 1 - i]
        gate, up = total[:, :wide], total[:, wide:]
        out_ref[i] = (gate / (1.0 + jnp.exp(-gate)) * up).astype(BF16)


def down_kernel(piece, blocks, far, n, begin, last, place_ref, scl_ref, codes_ref, *refs):
    me, group = place_ref[0], place_ref[3]
    hidden_refs, out_ref = refs[: len(blocks)], refs[-1]
    wide, depth, step = hidden_refs[0].shape[-1], codes_ref.shape[0], 2 * TILE
    units = wide // TILE
    for r in range(0, depth, step):
        total = None if begin else refs[len(blocks)][r : r + step]
        for q, hidden_ref in zip(blocks, hidden_refs):
            for i in range(2):
                block = (group * 2 + piece) * n + (me ^ q ^ (i * far))
                cols = pl.ds(pl.multiple_of(block * wide, TILE), wide)
                w = scaled(codes_ref[r : r + step, cols], lambda t, c: scl_ref[r // TILE + t, block * units + c], 2, units)
                part = lax.dot_general(w, hidden_ref[i], (((1,), (1,)), ((), ())), preferred_element_type=F32)
                total = part if total is None else total + part
        if not last:
            out_ref[r : r + step] = total
            continue
        total = total.T
        count, rows, _ = out_ref.shape
        for j in range(count):
            out_ref[j, :, r : r + step] = total[j * rows : (j + 1) * rows].astype(BF16)


def group_sum_kernel(got_ref, out_ref):
    n = out_ref.shape[0]
    for c in range(n):
        out_ref[c] = got_ref[c].astype(F32) + got_ref[n + c].astype(F32)


def final_kernel(place_ref, tok_ref, tok_mate_ref, branch_ref, branch_mate_ref, head_ref, head_mate_ref, out_ref, values_ref):
    n, rows, width = branch_ref.shape
    per = out_ref.shape[1] // width
    core = place_ref[1]
    total = jnp.zeros((rows, 1), F32)
    for side, (tok, head) in enumerate(((tok_ref, head_ref), (tok_mate_ref, head_mate_ref))):
        for i in range(per):
            cols = slice(i * width, (i + 1) * width)
            c = (core ^ side) * per + i
            branch = branch_ref[c] + branch_mate_ref[c]
            layer = (tok[:, cols].astype(F32) + branch).astype(BF16)
            if side == 0:
                out_ref[:, cols] = layer
            total = total + jnp.sum(layer.astype(F32) * head[:, cols], axis=-1, keepdims=True)
    row, at = (lax.broadcasted_iota(jnp.int32, (rows, rows), axis) for axis in (0, 1))
    taken = (row == at) & (row < place_ref[2])
    values_ref[...] = jnp.sum(jnp.where(taken, total, 0.0), axis=0, keepdims=True)


def call(kernel, name, ins, outs, limit=8, cost=None, scratch=()):
    specs = [x[1] if isinstance(x, tuple) else VMEM_SPEC for x in ins]
    return pl.pallas_call(
        kernel,
        in_specs=specs,
        out_specs=jax.tree.map(lambda _: VMEM_SPEC, outs),
        out_shape=outs,
        scratch_shapes=scratch,
        compiler_params=params(limit),
        cost_estimate=cost,
        name=name,
    )(*[x[0] if isinstance(x, tuple) else x for x in ins])


def body_split(n, tokens, lengths, norm_gain, gate_codes, gate_scales, up_codes, up_scales, down_codes, down_scales, value_head):
    rows, d_half = tokens.shape
    d, depth = 2 * d_half, gate_codes.shape[0]
    group_cols = gate_codes.shape[1] // 2
    units = group_cols // (2 * n * TILE)
    all_rows, half = 2 * n * rows, n // 2
    me, group, core = (lax.axis_index(a).astype(jnp.int32) for a in ("fsdp", "groups", "tp"))
    place = jnp.stack([me, core, lengths[0], group])
    spot = (place, SMEM_SPEC)
    shape = jax.ShapeDtypeStruct

    def swap(x, axis, bit):
        return lax.ppermute(x, axis, [(i, i ^ bit) for i in range(n if axis == "fsdp" else 2)])

    hbm = lambda x: pltpu.with_memory_space_constraint(x, pltpu.HBM)
    vmem = lambda x: pltpu.with_memory_space_constraint(x, pltpu.VMEM)
    unread = lambda x: (x, pl.BlockSpec(memory_space=pl.ANY))

    tok_mate = swap(tokens, "tp", 1)
    head = value_head.reshape(1, d_half)
    head_mate = swap(head, "tp", 1)
    whole = lambda x: (hbm(x), pl.BlockSpec())
    normed, gu_scales, down_scales = call(
        norm_kernel,
        "norm",
        [spot, whole(tokens), tok_mate]
        + [whole(a) for a in (norm_gain, gate_scales, up_scales, down_scales)]
        + [unread(head_mate)],
        [
            shape((2 * n, rows, depth), BF16),
            shape((2, *gate_scales.shape), F32),
            shape(down_scales.shape, F32),
        ],
    )
    normed = call(
        hold_kernel,
        "hold",
        [normed] + [unread(hbm(a)) for a in (gate_codes, up_codes, down_codes)],
        shape(normed.shape, BF16),
    )
    rows_axes = ("groups", "fsdp")
    x = call(
        rows_kernel,
        "rows",
        [lax.all_to_all(normed, rows_axes, 0, 0, tiled=True)],
        shape((all_rows, depth), BF16),
        scratch=[pltpu.VMEM((all_rows, depth), F32)],
    )

    wide = units * TILE
    codes = [vmem(c) for c in (gate_codes, up_codes)]
    cost = lambda share, width: pl.CostEstimate(
        flops=2 * all_rows * depth * width * n // share, transcendentals=0, bytes_accessed=2 * depth * width * n // share
    )

    coded = lambda count: shape((count * all_rows + CODE_ROWS, 2 * wide), jnp.int16)

    fars = (n // 2 + 2, n // 2 + 2)
    sums = shape((2, all_rows, 2 * wide), F32)

    def gate_up(name, after, *blocks):
        return call(
            functools.partial(gate_up_kernel, blocks, fars[blocks[0][0]], n),
            f"gate_up_{name}",
            [spot, (gu_scales, SMEM_SPEC), x, *codes, unread(after)],
            [coded(2) if q else sums for _, q in blocks],
            cost=cost(2, 2 * wide),
            scratch=[pltpu.VMEM(sums.shape, F32)],
        )

    orders = ((3, 1, 2), (3, 2, 1))
    sends_0 = gate_up("send_0", x, *[(0, q) for q in orders[0]])
    kept = gate_up("keep", sends_0[0], (0, 0), (1, 0))
    sends_1 = gate_up("send_1", kept[0], *[(1, q) for q in orders[1]])
    got = [[swap(send, "fsdp", q) for send, q in zip(sends_0, orders[0])]]
    branch = None
    both = [call(both_kernel, "both_0", [kept[0], *got[0]], [sums, coded(2)])]
    held = [call(hold_kernel, f"hold_send_{i}", [sends_1[i], unread(both[0][1])], coded(2)) for i in (1, 2)]
    got.append([swap(send, "fsdp", q) for send, q in zip((sends_1[0], *held), orders[1])])
    both.append(call(both_kernel, "both_1", [kept[1], *got[1], unread(hbm(down_codes))], [sums, coded(2)]))
    order = (1, 2, 3)
    for p in range(2):
        keep, send = both[p]
        hidden = call(hidden_kernel, f"hidden_{p}", [keep, swap(send, "fsdp", fars[p])], shape((2, all_rows, wide), BF16))
        branch = call(
            functools.partial(down_kernel, p, (0, *order), fars[p], n, p == 0, p == 1),
            f"down_{p}",
            [spot, (down_scales, SMEM_SPEC), vmem(down_codes), hidden]
            + [swap(hidden, "fsdp", q) for q in order]
            + ([branch] if p else []),
            shape((2 * n, rows, depth), BF16) if p else shape((depth, all_rows), F32),
            cost=cost(1, wide),
        )

    got = lax.all_to_all(branch, rows_axes, 0, 0, tiled=True)
    branch = call(group_sum_kernel, "group_sum", [got], shape((n, rows, depth), F32))
    layer_out, values = call(
        final_kernel,
        "final",
        [spot, tokens, tok_mate, branch, swap(branch, "tp", 1), head, head_mate],
        [shape((rows, d_half), BF16), shape((1, rows), F32)],
    )
    return layer_out, values.reshape(rows)


def solution(mesh):
    placed = (
        P(("groups", "fsdp"), "tp"),
        P(("groups", "fsdp")),
        P(),
        P("fsdp", "tp"),
        P("fsdp", "tp"),
        P("fsdp", "tp"),
        P("fsdp", "tp"),
        P("fsdp", "tp"),
        P("fsdp", "tp"),
        P("tp"),
    )
    n = mesh.shape["fsdp"]

    def body(*args):
        codes = args[3]
        fits = (
            n == 8
            and mesh.shape["groups"] == 2
            and mesh.shape["tp"] == 2
            and codes.shape[0] % (2 * TILE) == 0
            and codes.shape[1] == 8 * n * TILE
        )
        if fits:
            return body_split(n, *args)
        return body_any(*args)

    return jax.shard_map(
        body,
        mesh=mesh,
        in_specs=placed,
        out_specs=(P(("groups", "fsdp"), "tp"), P(("groups", "fsdp"))),
        check_vma=False,
    )
```
